128 devices in a mesh: row: 16 (over y, x), col: 8 (over z, core).
Axes of the slice: x: 4, y: 4, z: 4, core: 2. Of those that a mesh axis runs over, the one named last changes fastest.
Arguments:
- grad: bfloat16 [18432, 128, 128], P(('row', 'col')), may hold values from -6 to 6
- error: float32 [18432, 128, 128], P(('row', 'col')), may hold values from -4 to 4
- sel_blocks: int32 [128, 7], P(('row', 'col')), may hold values from 0 to 144, as said below
- row_bounds: int32 [17], replicated, may hold values from 0 to 24, as said below
- col_bounds: int32 [9], replicated, may hold values from 0 to 6, as said below
- master: float32 [256, 128, 128], P(('row', 'col')), may hold values from -6 to 6
- moment1: float32 [256, 128, 128], P(('row', 'col')), may hold values from -0.06 to 0.06
- moment2: float32 [256, 128, 128], P(('row', 'col')), may hold values from 1e-05 to 0.001
Outputs:
- error_out: float32 [18432, 128, 128], P(('row', 'col'))
- master_out: float32 [256, 128, 128], P(('row', 'col'))
- moment1_out: float32 [256, 128, 128], P(('row', 'col'))
- moment2_out: float32 [256, 128, 128], P(('row', 'col'))
- step_blocks: bfloat16 [144, 128, 128], replicated
The draws below stay inside these ranges and needn't reach their ends.
Inputs may be any that keep to these rules, and one draw needn't show every extreme that they name: `sel_blocks`: each row lists distinct block numbers below 144, then pads with 144; some row lists 7 blocks. `row_bounds`: starts at 0, never falls, ends at 24; a band holds 1 to 2 block rows and some band holds 2. `col_bounds`: starts at 0, never falls, ends at 6; a band holds 0 to 1 block columns and some band holds 1.
All inputs are finite; a program needn't handle non-finite values.
Results may differ from the reference program's by a relative error of at most 0.001.
Values may be sent and summed in bfloat16 or wider, within the bound.
No kernel may reach another device: no remote copies, remote signals or barrier semaphores. Data moves between devices by JAX's collectives and lax.ppermute only.
A program may use at most 128 MiB of HBM per device.

```python
import math
import jax
import jax.numpy as jnp
from jax import lax

BS = 128
CMAX = 1
GC = 6
TILE_NUMBER = 144
SEL = 7
OWNCAP = 2
N_ROW = 16
N_COL = 8


def band_starts(key, bands, raised, lowered):
    order = jax.random.permutation(key, bands)
    shifts = jnp.zeros((bands,), jnp.int32).at[order[:raised]].add(1).at[order[raised:raised + lowered]].add(-1)
    band_sizes = 1 + shifts
    return jnp.concatenate([jnp.zeros((1,), jnp.int32), jnp.cumsum(band_sizes).astype(jnp.int32)])


def draw_row_bounds(key, part):
    key = jax.random.fold_in(key, 21)
    return band_starts(key, N_ROW, N_ROW // 2, 0)


def draw_col_bounds(key, part):
    key = jax.random.fold_in(key, 37)
    return band_starts(key, N_COL, 0, N_COL // 4)


def draw_sel_blocks(key, part):
    key = jax.random.fold_in(key, 11)
    worker_sequence = N_ROW * N_COL
    favored_random_seed, rating_random_seed, extra_random_seed, tally_random_seed, entire_random_seed = jax.random.split(key, 5)
    favored_tiles = jax.random.randint(favored_random_seed, (TILE_NUMBER,), 0, 2)
    tile_ranking = jax.random.randint(rating_random_seed, (worker_sequence, TILE_NUMBER), 0, 1024)
    tile_ranking = tile_ranking + 1024 * favored_tiles[None, :] * jax.random.randint(extra_random_seed, (worker_sequence, TILE_NUMBER), 0, 2)
    tile_ranking = tile_ranking * TILE_NUMBER + jnp.arange(TILE_NUMBER, dtype=jnp.int32)[None, :]
    ignored, picked = lax.top_k(tile_ranking, SEL)
    counts = jax.random.randint(tally_random_seed, (worker_sequence,), 1, SEL + 1)
    fullest = jax.random.randint(entire_random_seed, (), 0, worker_sequence)
    counts = jnp.where(jnp.arange(worker_sequence) == fullest, SEL, counts)
    keep = jnp.arange(SEL)[None, :] < counts[:, None]
    return jnp.where(keep, picked, TILE_NUMBER).astype(jnp.int32)


def levels(own_key, shape, cuts, smallest, largest):
    level, own = 1.0, jax.random.fold_in(own_key, 6)
    for dim, shards_of in cuts:
        draws = jnp.exp(jax.random.uniform(jax.random.fold_in(own, dim), (shards_of,), jnp.float32, smallest / len(cuts), largest / len(cuts)))
        level = level * jnp.repeat(draws, shape[dim] // shards_of).reshape([-1 if axis == dim else 1 for axis in range(len(shape))])
    return level


def gaussian(stream_key, extent, deviation, bound, cuts=(), kind=jnp.bfloat16):
    gain = levels(stream_key, extent, cuts, -0.22, 0.18) if cuts else 1.0
    entries = jax.random.normal(stream_key, extent, jnp.float32) * deviation * gain
    return jnp.minimum(jnp.maximum(entries, -bound), bound).astype(kind)


def setup_inputs(seed: int = 0) -> dict:
    seeds = jax.random.split(jax.random.key(seed), 9)
    grad = gaussian(seeds[0], (N_ROW * N_COL * TILE_NUMBER, BS, BS), 1.0, 6.0, ((0, 128),))
    error = gaussian(seeds[1], (N_ROW * N_COL * TILE_NUMBER, BS, BS), 0.5, 4.0, ((0, 128),), jnp.float32)
    sel_blocks = draw_sel_blocks(jax.random.fold_in(seeds[8], 71), 0)
    row_bounds = draw_row_bounds(jax.random.fold_in(seeds[8], 71), 0)
    col_bounds = draw_col_bounds(jax.random.fold_in(seeds[8], 71), 0)
    master = gaussian(seeds[5], (N_ROW * N_COL * OWNCAP, BS, BS), 1.0, 6.0, ((0, 128),), jnp.float32)
    moment1 = gaussian(seeds[6], (N_ROW * N_COL * OWNCAP, BS, BS), 0.01, 0.06, ((0, 128),), jnp.float32)
    moment2 = jnp.clip(jnp.exp(math.log(0.001) - 4.6051703 * jax.random.uniform(seeds[7], (N_ROW * N_COL * OWNCAP, BS, BS), jnp.float32) ** levels(seeds[7], (N_ROW * N_COL * OWNCAP, BS, BS), ((0, 128),), -0.2, 0.2)), 9.999999747378752e-06, 0.001)
    return dict(grad=grad, error=error, sel_blocks=sel_blocks, row_bounds=row_bounds, col_bounds=col_bounds, master=master, moment1=moment1, moment2=moment2)


BETA_ONE = 0.9
BETA_TWO = 0.95
EPSILON = 1e-08
DECAY_RATE = 0.1
LEARN_RATE = 0.01
CORRECT_ONE = 1.0 - 0.9 ** 10
CORRECT_TWO = 1.0 - 0.95 ** 10

def band_of(bounds, positions):
    inner_cuts = bounds[1:-1]
    return lax.optimization_barrier(jnp.sum((inner_cuts[None, :] <= positions[:, None]).astype(jnp.int32), axis=1))

def adamw_update(totals, master, moment1, moment2, worker_sequence):
    averaged = totals / worker_sequence
    first = BETA_ONE * moment1 + (1.0 - BETA_ONE) * averaged
    second = BETA_TWO * moment2 + (1.0 - BETA_TWO) * averaged * averaged
    direction = first / CORRECT_ONE / (jnp.sqrt(second / CORRECT_TWO) + EPSILON) + DECAY_RATE * master
    return (master - LEARN_RATE * direction, first, second, direction)

def reference(grad, error, sel_blocks, row_bounds, col_bounds, master, moment1, moment2):
    worker_sequence = N_ROW * N_COL
    grads = grad.reshape(worker_sequence, TILE_NUMBER, BS, BS)
    errors = error.reshape(worker_sequence, TILE_NUMBER, BS, BS)
    blocks = jnp.arange(TILE_NUMBER, dtype=jnp.int32)

    def visit_device(carry, inputs):
        totals, tallies = carry
        grad_part, error_part, picked = inputs
        accumulated = grad_part.astype(jnp.float32) + error_part
        chosen = lax.optimization_barrier(jnp.sum((picked[:, None] == blocks[None, :]).astype(jnp.float32), axis=0))
        carry_next = (totals + accumulated * chosen[:, None, None], tallies + chosen)
        return (carry_next, accumulated * (1.0 - chosen)[:, None, None])
    start_carry = (jnp.zeros((TILE_NUMBER, BS, BS), jnp.float32), jnp.zeros((TILE_NUMBER,), jnp.float32))
    (totals, tallies), residuals = lax.scan(visit_device, start_carry, (grads, errors, sel_blocks))
    error_out = residuals.reshape(worker_sequence * TILE_NUMBER, BS, BS)
    slot_ids = jnp.arange(worker_sequence * OWNCAP, dtype=jnp.int32)
    owner_of = slot_ids // OWNCAP
    offset_in = slot_ids % OWNCAP
    band_row = owner_of // N_COL
    band_col = owner_of % N_COL
    grid_row = row_bounds[band_row] + offset_in // CMAX
    grid_col = col_bounds[band_col] + offset_in % CMAX
    inside = (grid_row < row_bounds[band_row + 1]) & (grid_col < col_bounds[band_col + 1])
    target = jnp.where(inside, grid_row * GC + grid_col, 0)
    gathered = totals[target]
    counted = tallies[target]
    changed = inside & (counted > 0.5)
    new_master, first, second, direction = adamw_update(gathered, master, moment1, moment2, worker_sequence)
    flags = changed[:, None, None]
    master_out = jnp.where(flags, new_master, master)
    moment1_out = jnp.where(flags, first, moment1)
    moment2_out = jnp.where(flags, second, moment2)
    step_slots = jnp.where(flags, direction, 0.0).astype(jnp.bfloat16)
    block_row = blocks // GC
    block_col = blocks % GC
    row_band = band_of(row_bounds, block_row)
    col_band = band_of(col_bounds, block_col)
    slot_of = (row_band * N_COL + col_band) * OWNCAP + (block_row - row_bounds[row_band]) * CMAX + (block_col - col_bounds[col_band])
    step_blocks = step_slots[slot_of]
    return (error_out, master_out, moment1_out, moment2_out, step_blocks)
```

```python
import jax
import jax.numpy as jnp
from jax import lax
from jax.experimental import pallas as pl
from jax.experimental.pallas import tpu as pltpu
from jax.sharding import Mesh
from jax.sharding import PartitionSpec as P

BS = 128
GC = 6
GR = 24
BLOCKS = 144
SEL = 7
OWNCAP = 2
N_ROW = 16
N_COL = 8
DEVICES = N_ROW * N_COL
CHIPS = DEVICES // 2
HALF = BS // 2

MSG = 16
ID_ROW = SEL
STATE_ROW = 8
EXT = 16
OUT_MSG = BLOCKS + EXT

BETA_ONE = 0.9
BETA_TWO = 0.95
EPSILON = 1e-08
DECAY_RATE = 0.1
LEARN_RATE = 0.01
CORRECT_ONE = 1.0 - 0.9**10
CORRECT_TWO = 1.0 - 0.95**10

F32 = jnp.float32
BF16 = jnp.bfloat16
I32 = jnp.int32
SMEM = pl.BlockSpec(memory_space=pltpu.SMEM)
VMEM = pl.BlockSpec(memory_space=pltpu.VMEM)
VMEM_LIMIT = 40 * 1024 * 1024


def adamw(totals, master, moment1, moment2):
    averaged = totals / DEVICES
    first = BETA_ONE * moment1 + (1.0 - BETA_ONE) * averaged
    second = BETA_TWO * moment2 + (1.0 - BETA_TWO) * averaged * averaged
    direction = first / CORRECT_ONE / (jnp.sqrt(second / CORRECT_TWO) + EPSILON) + DECAY_RATE * master
    return first, second, direction


def three_terms(x):
    high = x.astype(BF16)
    rest = x - high.astype(F32)
    middle = rest.astype(BF16)
    low = (rest - middle.astype(F32)).astype(BF16)
    return high, middle, low


def pack_kernel(sel_ref, *refs):
    grads, errors = refs[:SEL], refs[SEL : 2 * SEL]
    master, moment1, moment2, send = refs[2 * SEL :]

    def put(row, block):
        for core in range(2):
            send[pl.ds(core * MSG + row, CHIPS, stride=2 * MSG), :] = block[core * HALF : (core + 1) * HALF]

    for k in range(SEL):
        put(k, grads[k][0].astype(F32) + errors[k][0])
    lane = lax.broadcasted_iota(I32, (HALF, BS), 1)
    ids = jnp.zeros((HALF, BS), I32)
    for k in range(SEL):
        ids = jnp.where(lane == k, sel_ref[0, k], ids)
    ids = ids.astype(F32)
    put(ID_ROW, jnp.concatenate([ids, ids], axis=0))
    for s in range(OWNCAP):
        put(STATE_ROW + s, moment1[s])
        put(STATE_ROW + 2 + s, moment2[s])
        put(STATE_ROW + 4 + s, master[s])
    for row in (STATE_ROW + 6, STATE_ROW + 7):
        put(row, jnp.zeros((BS, BS), F32))


def pack(sel, grad, error, master, moment1, moment2):
    def chosen(k):
        return pl.BlockSpec((1, BS, BS), lambda i, sel_ref: (jnp.minimum(sel_ref[0, k], BLOCKS - 1), 0, 0))

    whole = pl.BlockSpec((OWNCAP, BS, BS), lambda i, sel_ref: (0, 0, 0))
    return pl.pallas_call(
        pack_kernel,
        grid_spec=pltpu.PrefetchScalarGridSpec(
            num_scalar_prefetch=1,
            grid=(1,),
            in_specs=[chosen(k) for k in range(SEL)] * 2 + [whole] * 3,
            out_specs=pl.BlockSpec((DEVICES * MSG, BS), lambda i, sel_ref: (0, 0)),
        ),
        out_shape=jax.ShapeDtypeStruct((DEVICES * MSG, BS), F32),
        compiler_params=pltpu.CompilerParams(vmem_limit_bytes=VMEM_LIMIT),
        cost_estimate=pl.CostEstimate(flops=200_000, bytes_accessed=2_200_000, transcendentals=0),
        name="pack_rows",
    )(sel, *[grad] * SEL, *[error] * SEL, master, moment1, moment2)


FEED = 8


def feedback_kernel(sel_ref, grad, error, out):
    first = pl.program_id(0) * FEED
    for b in range(FEED):
        hit = sel_ref[0, 0] == first + b
        for k in range(1, SEL):
            hit = jnp.logical_or(hit, sel_ref[0, k] == first + b)
        keep = 1.0 - hit.astype(F32)
        out[b] = (grad[b].astype(F32) + error[b]) * keep


def feedback(sel, grad, error):
    block = pl.BlockSpec((FEED, BS, BS), lambda i: (i, 0, 0))
    return pl.pallas_call(
        feedback_kernel,
        grid=(BLOCKS // FEED,),
        in_specs=[SMEM, block, block],
        out_specs=block,
        out_shape=jax.ShapeDtypeStruct((BLOCKS, BS, BS), F32),
        compiler_params=pltpu.CompilerParams(vmem_limit_bytes=VMEM_LIMIT),
        cost_estimate=pl.CostEstimate(flops=5_000_000, bytes_accessed=23_600_000, transcendentals=0),
        name="error_feedback",
    )(sel, grad, error)


def band(cuts, bands, positions):
    index = jnp.zeros_like(positions)
    start = jnp.zeros_like(positions)
    for k in range(1, bands):
        past = cuts[k] <= positions
        index = index + past.astype(I32)
        start = jnp.where(past, cuts[k], start)
    return index, start


def maps_kernel(place_ref, rows_ref, cols_ref, slot_map, block_map):
    block = lax.broadcasted_iota(I32, (BLOCKS, BS), 0)
    lane = lax.broadcasted_iota(I32, (BLOCKS, BS), 1)
    grid_row = block // GC
    grid_col = block - grid_row * GC
    row_band, row_start = band(rows_ref, N_ROW, grid_row)
    col_band, col_start = band(cols_ref, N_COL, grid_col)
    owner = row_band * N_COL + col_band
    slot = (grid_row - row_start) + (grid_col - col_start)
    for s in range(OWNCAP):
        slot_map[:, s * BS : (s + 1) * BS] = jnp.where((owner == lane) & (slot == s), 1.0, 0.0).astype(BF16)
    core = place_ref[0]
    chip = lax.broadcasted_iota(I32, (CHIPS, BS), 0)
    for t in range(2 * OWNCAP):
        holder = 2 * chip + (core if t < OWNCAP else 1 - core)
        band_row = holder // N_COL
        band_col = holder - band_row * N_COL
        top = jnp.zeros_like(chip)
        end = jnp.zeros_like(chip)
        for k in range(N_ROW):
            top = jnp.where(band_row == k, rows_ref[k], top)
            end = jnp.where(band_row == k, rows_ref[k + 1], end)
        left = jnp.zeros_like(chip)
        right = jnp.zeros_like(chip)
        for k in range(N_COL):
            left = jnp.where(band_col == k, cols_ref[k], left)
            right = jnp.where(band_col == k, cols_ref[k + 1], right)
        at_row = top + t % OWNCAP
        target = jnp.where((at_row < end) & (left < right), at_row * GC + left, -1)
        for part in range(2):
            lane = lax.broadcasted_iota(I32, (CHIPS, BS), 1) + part * BS
            block_map[t * CHIPS : (t + 1) * CHIPS, part * BS : (part + 1) * BS] = jnp.where(
                target == lane, 1.0, 0.0
            ).astype(BF16)


def maps(place, row_bounds, col_bounds):
    return pl.pallas_call(
        maps_kernel,
        in_specs=[SMEM] * 3,
        out_specs=[VMEM] * 2,
        out_shape=[
            jax.ShapeDtypeStruct((BLOCKS, OWNCAP * BS), BF16),
            jax.ShapeDtypeStruct((2 * OWNCAP * CHIPS, 2 * BS), BF16),
        ],
        cost_estimate=pl.CostEstimate(flops=500_000, bytes_accessed=300_000, transcendentals=0),
        name="slot_maps",
    )(place, row_bounds, col_bounds)


def directions_kernel(place_ref, rows_ref, cols_ref, got, slot_map, block_map, message, flags, tally_ref, ext):
    def rows(k):
        return got[pl.ds(k, DEVICES, stride=MSG), :]

    ids = jnp.transpose(rows(ID_ROW))
    block = lax.broadcasted_iota(I32, (BLOCKS, DEVICES), 0).astype(F32)
    picks = jnp.concatenate(
        [jnp.where(ids[k : k + 1] == block, 1.0, 0.0).astype(BF16) for k in range(SEL)], axis=1
    )
    values = jnp.concatenate([rows(k) for k in range(SEL)], axis=0)
    ones = jnp.ones((SEL * DEVICES, BS), BF16)
    sums = jnp.dot(picks, jnp.concatenate([*three_terms(values), ones], axis=1), preferred_element_type=F32)
    totals = (sums[:, :BS] + sums[:, BS : 2 * BS]) + sums[:, 2 * BS : 3 * BS]
    tallies = sums[:, 3 * BS :]
    tally_ref[...] = tallies

    states = []
    for array in range(3):
        held = jnp.concatenate([rows(STATE_ROW + 2 * array + s) for s in range(OWNCAP)], axis=0)
        states += three_terms(held)
    found = jnp.dot(slot_map[...], jnp.concatenate(states, axis=1), preferred_element_type=F32)
    term = [found[:, n * BS : (n + 1) * BS] for n in range(9)]
    moment1, moment2, master = [(term[3 * a] + term[3 * a + 1]) + term[3 * a + 2] for a in range(3)]

    direction = adamw(totals, master, moment1, moment2)[2]
    direction = jnp.where(tallies > 0.5, direction, 0.0).astype(BF16)
    for i in range(CHIPS):
        message[i, :BLOCKS] = direction

    padded = jnp.concatenate([totals, jnp.zeros((2 * BS - BLOCKS, BS), F32)], axis=0)
    owned = jnp.dot(block_map[...], jnp.concatenate(three_terms(padded), axis=1), preferred_element_type=F32)
    for p in range(3):
        for t in range(2 * OWNCAP):
            ext[pl.ds(2 * OWNCAP * p + t, CHIPS, stride=EXT), :] = owned[
                t * CHIPS : (t + 1) * CHIPS, p * BS : (p + 1) * BS
            ]
    for row in range(6 * OWNCAP, EXT):
        ext[pl.ds(row, CHIPS, stride=EXT), :] = jnp.zeros((CHIPS, BS), F32)
    for i in range(CHIPS):
        message[i, BLOCKS:] = ext[i * EXT : (i + 1) * EXT].astype(BF16)

    band_row = place_ref[1]
    band_col = place_ref[2]
    left = cols_ref[band_col]
    flags[...] = jnp.zeros_like(flags)
    for s in range(OWNCAP):
        at_row = rows_ref[band_row] + s
        inside = (at_row < rows_ref[band_row + 1]) & (left < cols_ref[band_col + 1])
        target = jnp.where(inside, at_row * GC + left, 0)
        flags[s : s + 1] = tally_ref[pl.ds(target, 1), :] * inside.astype(F32)


def directions(place, row_bounds, col_bounds, got, slot_map, block_map):
    return pl.pallas_call(
        directions_kernel,
        in_specs=[SMEM] * 3 + [VMEM] * 3,
        out_specs=[VMEM] * 2,
        out_shape=[
            jax.ShapeDtypeStruct((CHIPS, OUT_MSG, BS), BF16),
            jax.ShapeDtypeStruct((8, BS), F32),
        ],
        scratch_shapes=[pltpu.VMEM((BLOCKS, BS), F32), pltpu.VMEM((CHIPS * EXT, BS), F32)],
        compiler_params=pltpu.CompilerParams(vmem_limit_bytes=VMEM_LIMIT),
        cost_estimate=pl.CostEstimate(flops=200_000_000, bytes_accessed=4_000_000, transcendentals=20_000),
        name="directions",
    )(place, row_bounds, col_bounds, got, slot_map, block_map)


GROUP = 16


def turn(rows, out, scratch):
    scratch[...] = rows[...].astype(F32).reshape(CHIPS * GROUP, BS)
    for b in range(GROUP):
        out[b] = scratch[pl.ds(b, CHIPS, stride=GROUP), :].astype(BF16)


def own_half_kernel(place_ref, rows, out, scratch):
    turn(rows, out, scratch)


def own_half(place, mine):
    return pl.pallas_call(
        own_half_kernel,
        grid_spec=pltpu.PrefetchScalarGridSpec(
            num_scalar_prefetch=1,
            grid=(BLOCKS // GROUP,),
            in_specs=[pl.BlockSpec((CHIPS, GROUP, BS), lambda g, place_ref: (0, g, 0))],
            out_specs=pl.BlockSpec((GROUP, HALF, BS), lambda g, place_ref: (g, place_ref[0], 0)),
            scratch_shapes=[pltpu.VMEM((CHIPS * GROUP, BS), F32)],
        ),
        out_shape=jax.ShapeDtypeStruct((BLOCKS, BS, BS), BF16),
        compiler_params=pltpu.CompilerParams(vmem_limit_bytes=VMEM_LIMIT),
        cost_estimate=pl.CostEstimate(flops=2_000_000, bytes_accessed=4_700_000, transcendentals=0),
        name="own_half",
    )(place, mine)


def other_half_kernel(
    place_ref, steps, rows, mine_ext, theirs_ext, flags, master, moment1, moment2,
    out, master_out, moment1_out, moment2_out, scratch, totals,
):
    turn(rows, out, scratch)

    @pl.when(pl.program_id(0) == BLOCKS // GROUP - 1)
    def _():
        core = place_ref[0]
        for own, ext in ((True, mine_ext), (False, theirs_ext)):
            scratch[...] = ext[...].astype(F32).reshape(CHIPS * EXT, BS)
            at = pl.multiple_of((core if own else 1 - core) * HALF, HALF)
            for s in range(OWNCAP):
                first = s if own else OWNCAP + s
                part = [scratch[pl.ds(2 * OWNCAP * p + first, CHIPS, stride=EXT), :] for p in range(3)]
                totals[s, pl.ds(at, HALF), :] = (part[0] + part[1]) + part[2]
        for s in range(OWNCAP):
            changed = flags[s : s + 1] > 0.5
            new1, new2, direction = adamw(totals[s], master[s], moment1[s], moment2[s])
            master_out[s] = jnp.where(changed, master[s] - LEARN_RATE * direction, master[s])
            moment1_out[s] = jnp.where(changed, new1, moment1[s])
            moment2_out[s] = jnp.where(changed, new2, moment2[s])


def other_half(place, steps, mine, theirs, flags, master, moment1, moment2):
    ext = pl.BlockSpec((CHIPS, EXT, BS), lambda g, place_ref: (0, BLOCKS // EXT, 0))
    state = pl.BlockSpec((OWNCAP, BS, BS), lambda g, place_ref: (0, 0, 0))
    slots = jax.ShapeDtypeStruct((OWNCAP, BS, BS), F32)
    return pl.pallas_call(
        other_half_kernel,
        grid_spec=pltpu.PrefetchScalarGridSpec(
            num_scalar_prefetch=1,
            grid=(BLOCKS // GROUP,),
            in_specs=[
                pl.BlockSpec(memory_space=pl.ANY),
                pl.BlockSpec((CHIPS, GROUP, BS), lambda g, place_ref: (0, g, 0)),
                ext,
                ext,
                pl.BlockSpec((8, BS), lambda g, place_ref: (0, 0)),
                state,
                state,
                state,
            ],
            out_specs=[
                pl.BlockSpec((GROUP, HALF, BS), lambda g, place_ref: (g, 1 - place_ref[0], 0)),
                state,
                state,
                state,
            ],
            scratch_shapes=[pltpu.VMEM((CHIPS * GROUP, BS), F32), pltpu.VMEM((OWNCAP, BS, BS), F32)],
        ),
        out_shape=[jax.ShapeDtypeStruct((BLOCKS, BS, BS), BF16), slots, slots, slots],
        input_output_aliases={1: 0},
        compiler_params=pltpu.CompilerParams(vmem_limit_bytes=VMEM_LIMIT),
        cost_estimate=pl.CostEstimate(flops=3_000_000, bytes_accessed=6_500_000, transcendentals=0),
        name="other_half",
    )(place, steps, theirs, mine, theirs, flags, master, moment1, moment2)


def local(grad, error, sel_blocks, row_bounds, col_bounds, master, moment1, moment2):
    row, z, core = lax.axis_index("row"), lax.axis_index("z"), lax.axis_index("core")
    place = jnp.stack([core, row, 2 * z + core]).astype(I32)
    send = pack(sel_blocks, grad, error, master, moment1, moment2)
    got = lax.all_to_all(send, ("row", "z", "core"), split_axis=0, concat_axis=0, tiled=True)
    error_out = feedback(sel_blocks, grad, error)
    slot_map, block_map = maps(place, row_bounds, col_bounds)
    message, flags = directions(place, row_bounds, col_bounds, got, slot_map, block_map)
    mine = lax.all_to_all(
        message.reshape(CHIPS * OUT_MSG, BS), ("row", "z"), split_axis=0, concat_axis=0, tiled=True
    )
    theirs = lax.ppermute(mine, "core", [(0, 1), (1, 0)])
    mine = mine.reshape(CHIPS, OUT_MSG, BS)
    theirs = theirs.reshape(CHIPS, OUT_MSG, BS)
    steps = own_half(place, mine)
    steps, master_out, moment1_out, moment2_out = other_half(
        place, steps, mine, theirs, flags, master, moment1, moment2
    )
    return (error_out, master_out, moment1_out, moment2_out, steps)


def solution(mesh):
    cores = Mesh(mesh.devices.reshape(N_ROW, N_COL // 2, 2), ("row", "z", "core"))
    split = P(("row", "z", "core"))
    return jax.shard_map(
        local,
        mesh=cores,
        in_specs=(split, split, split, P(), P(), split, split, split),
        out_specs=(split, split, split, split, P()),
        check_vma=False,
    )
```

```python
import jax
import jax.numpy as jnp
from jax import lax
from jax.experimental import pallas as pl
from jax.experimental.pallas import tpu as pltpu
from jax.sharding import Mesh
from jax.sharding import PartitionSpec as P

BS = 128
GC = 6
GR = 24
BLOCKS = 144
SEL = 7
OWNCAP = 2
N_ROW = 16
N_COL = 8
DEVICES = N_ROW * N_COL
PLANE = N_ROW

MSG = 8
STATE_ROW = 4
INFO_ROW = 7
SCALE_LANE = 8
UNIT = 2.0**26
STEPS = 32767.0
ROOT_STEPS = 65535.0
ROOT_LOW = 32768.0

BETA_ONE = 0.9
BETA_TWO = 0.95
EPSILON = 1e-08
DECAY_RATE = 0.1
LEARN_RATE = 0.01
CORRECT_ONE = 1.0 - 0.9**10
CORRECT_TWO = 1.0 - 0.95**10

F32 = jnp.float32
BF16 = jnp.bfloat16
I32 = jnp.int32
SMEM = pl.BlockSpec(memory_space=pltpu.SMEM)
VMEM = pl.BlockSpec(memory_space=pltpu.VMEM)
HBM = pl.BlockSpec(memory_space=pltpu.HBM)
ANY = pl.BlockSpec(memory_space=pl.ANY)
MIB = 1024 * 1024
PARAMS = pltpu.CompilerParams(vmem_limit_bytes=16 * MIB)
ALONE = pltpu.CompilerParams(vmem_limit_bytes=64 * MIB)
NEARLY_ALONE = pltpu.CompilerParams(vmem_limit_bytes=61 * MIB)


def adamw(totals, master, moment1, moment2):
    averaged = totals / DEVICES
    first = BETA_ONE * moment1 + (1.0 - BETA_ONE) * averaged
    second = BETA_TWO * moment2 + (1.0 - BETA_TWO) * averaged * averaged
    direction = first / CORRECT_ONE / (jnp.sqrt(second / CORRECT_TWO) + EPSILON) + DECAY_RATE * master
    return first, second, direction


def three_terms(x):
    high = x.astype(BF16)
    rest = x - high.astype(F32)
    middle = rest.astype(BF16)
    low = (rest - middle.astype(F32)).astype(BF16)
    return high, middle, low


def first_row(z, core):
    return core * (BS // 2) + z * PLANE


def pack_kernel(sel_hbm, grad, error, master, moment1, moment2, send, sel, grads, errors, states, sel_sem, sems):
    fetch_sel = pltpu.make_async_copy(sel_hbm, sel, sel_sem)
    fetch_sel.start()
    held = [
        pltpu.make_async_copy(array, states.at[n], sems.at[2 * SEL + n])
        for n, array in enumerate((moment1, moment2, master))
    ]
    for copy in held:
        copy.start()
    fetch_sel.wait()
    chosen = []
    for k in range(SEL):
        at = jnp.minimum(sel[0, k], BLOCKS - 1)
        chosen.append(pltpu.make_async_copy(grad.at[at], grads.at[k], sems.at[k]))
        chosen.append(pltpu.make_async_copy(error.at[at], errors.at[k], sems.at[SEL + k]))
    for copy in chosen:
        copy.start()

    def put(row, block):
        for col in range(N_COL):
            at = first_row(col // 2, col % 2)
            send[pl.ds(col * MSG + row, PLANE, stride=N_COL * MSG), :] = block[at : at + PLANE]

    lane = lax.broadcasted_iota(I32, (BS, BS), 1)
    info = jnp.zeros((BS, BS), I32)
    for k in range(SEL):
        info = jnp.where(lane == k, sel[0, k], info)

    def coded(n, info, block, root=False):
        scale = jnp.maximum(jnp.ceil(jnp.max(jnp.abs(block), axis=1, keepdims=True) * UNIT), 1.0)
        info = jnp.where(lane == SCALE_LANE + n, scale.astype(I32), info)
        if root:
            return jnp.round(block * (ROOT_STEPS * UNIT / scale) - ROOT_LOW).astype(I32), info
        return jnp.round(block * (STEPS * UNIT / scale)).astype(I32), info

    def put_pair(row, first, second):
        put(row, lax.shift_left(first, 16) | (second & 0xFFFF))

    for n in range(3):
        held[n].wait()
        pair = []
        for s in range(OWNCAP):
            block = states[n, s]
            code, info = coded(SEL + OWNCAP * n + s, info, jnp.sqrt(block) if n == 1 else block, n == 1)
            pair.append(code)
        put_pair(STATE_ROW + n, *pair)
    pair = []
    for k in range(SEL):
        chosen[2 * k].wait()
        chosen[2 * k + 1].wait()
        code, info = coded(k, info, grads[k].astype(F32) + errors[k])
        pair.append(code)
        if len(pair) == 2:
            put_pair(k // 2, *pair)
            pair = []
    put_pair(SEL // 2, pair[0], jnp.zeros((BS, BS), I32))
    put(INFO_ROW, info)


def pack(sel, grad, error, master, moment1, moment2):
    return pl.pallas_call(
        pack_kernel,
        in_specs=[HBM] * 6,
        out_specs=VMEM,
        out_shape=jax.ShapeDtypeStruct((DEVICES * MSG, BS), I32),
        scratch_shapes=[
            pltpu.SMEM((1, SEL), I32),
            pltpu.VMEM((SEL, BS, BS), BF16),
            pltpu.VMEM((SEL, BS, BS), F32),
            pltpu.VMEM((3, OWNCAP, BS, BS), F32),
            pltpu.SemaphoreType.DMA,
            pltpu.SemaphoreType.DMA((2 * SEL + 3,)),
        ],
        compiler_params=ALONE,
        cost_estimate=pl.CostEstimate(flops=200_000, bytes_accessed=2_200_000, transcendentals=0),
        name="pack_rows",
    )(sel, grad, error, master, moment1, moment2)


def band(cuts, bands, positions):
    index = jnp.zeros_like(positions)
    start = jnp.zeros_like(positions)
    for k in range(1, bands):
        past = cuts[k] <= positions
        index = index + past.astype(I32)
        start = jnp.where(past, cuts[k], start)
    return index, start


FEED = 18


def feedback(sel, grad, error, part, before):
    steps = BLOCKS // FEED // 2

    def kernel(*refs):
        sel, grad, error, out = *refs[:3], refs[-1]

        def step(grad_blocks, error_blocks, out_blocks):
            first = (part * steps + pl.program_id(0)) * FEED
            for b in range(FEED):
                hit = sel[0, 0] == first + b
                for k in range(1, SEL):
                    hit = jnp.logical_or(hit, sel[0, k] == first + b)
                keep = 1.0 - hit.astype(F32)
                out_blocks[b] = (grad_blocks[b].astype(F32) + error_blocks[b]) * keep

        block = pl.BlockSpec((FEED, BS, BS), lambda i: (part * steps + i, 0, 0))
        pltpu.emit_pipeline(step, grid=(steps,), in_specs=[block, block], out_specs=[block])(grad, error, out)

    more = [] if before is None else [before]
    return pl.pallas_call(
        kernel,
        in_specs=[SMEM] + [HBM] * 2 + [HBM] * len(more),
        out_specs=HBM,
        out_shape=jax.ShapeDtypeStruct((BLOCKS, BS, BS), F32),
        input_output_aliases={3: 0} if more else {},
        compiler_params=NEARLY_ALONE,
        cost_estimate=pl.CostEstimate(flops=2_500_000, bytes_accessed=11_800_000, transcendentals=0),
        name="error_feedback",
    )(sel, grad, error, *more)


def maps_kernel(rows_ref, cols_ref, slot_map, block_map, own_map):
    block = lax.broadcasted_iota(I32, (BLOCKS, BS), 0)
    lane = lax.broadcasted_iota(I32, (BLOCKS, BS), 1)
    grid_row = block // GC
    grid_col = block - grid_row * GC
    row_band, row_start = band(rows_ref, N_ROW, grid_row)
    col_band, col_start = band(cols_ref, N_COL, grid_col)
    owner = row_band * N_COL + col_band
    slot = (grid_row - row_start) + (grid_col - col_start)
    for s in range(OWNCAP):
        slot_map[:, s * BS : (s + 1) * BS] = jnp.where((owner == lane) & (slot == s), 1.0, 0.0).astype(BF16)
    holder = lax.broadcasted_iota(I32, (DEVICES * OWNCAP, BS), 0)
    slot = holder % OWNCAP
    holder = holder // OWNCAP
    band_row = holder // N_COL
    band_col = holder - band_row * N_COL
    top = jnp.zeros_like(holder)
    end = jnp.zeros_like(holder)
    for k in range(N_ROW):
        top = jnp.where(band_row == k, rows_ref[k], top)
        end = jnp.where(band_row == k, rows_ref[k + 1], end)
    left = jnp.zeros_like(holder)
    right = jnp.zeros_like(holder)
    for k in range(N_COL):
        left = jnp.where(band_col == k, cols_ref[k], left)
        right = jnp.where(band_col == k, cols_ref[k + 1], right)
    at_row = top + slot
    target = jnp.where((at_row < end) & (left < right), at_row * GC + left, -1)
    lane = lax.broadcasted_iota(I32, (DEVICES * OWNCAP, BS), 1)
    for part in range(2):
        block_map[:, part * BS : (part + 1) * BS] = jnp.where(target == lane + part * BS, 1.0, 0.0).astype(BF16)
    band_row = lax.axis_index("row")
    band_col = 2 * lax.axis_index("z") + lax.axis_index("core")
    slot = lax.broadcasted_iota(I32, (16, 2 * BS), 0)
    at_row = rows_ref[band_row] + slot
    left = cols_ref[band_col]
    inside = (slot < OWNCAP) & (at_row < rows_ref[band_row + 1]) & (left < cols_ref[band_col + 1])
    lane = lax.broadcasted_iota(I32, (16, 2 * BS), 1)
    own_map[...] = jnp.where(inside & (at_row * GC + left == lane), 1.0, 0.0).astype(BF16)


def maps(row_bounds, col_bounds):
    return pl.pallas_call(
        maps_kernel,
        in_specs=[SMEM] * 2,
        out_specs=[VMEM] * 3,
        out_shape=[
            jax.ShapeDtypeStruct((BLOCKS, OWNCAP * BS), BF16),
            jax.ShapeDtypeStruct((OWNCAP * DEVICES, 2 * BS), BF16),
            jax.ShapeDtypeStruct((16, 2 * BS), BF16),
        ],
        compiler_params=PARAMS,
        cost_estimate=pl.CostEstimate(flops=500_000, bytes_accessed=300_000, transcendentals=0),
        name="slot_maps",
    )(row_bounds, col_bounds)


def directions_kernel(got, slot_map, block_map, own_map, message, owned, flags):
    def rows(k):
        return got[pl.ds(k, DEVICES, stride=MSG), :]

    info = rows(INFO_ROW)

    def decoded(row, n):
        words = rows(row)
        for half in (lax.shift_right_arithmetic(words, 16), lax.shift_right_arithmetic(lax.shift_left(words, 16), 16)):
            if n < SEL or row > SEL // 2:
                scale = info[:, SCALE_LANE + n : SCALE_LANE + n + 1].astype(F32)
                if row == STATE_ROW + 1:
                    yield (half.astype(F32) + ROOT_LOW) * (scale * (1.0 / (ROOT_STEPS * UNIT)))
                else:
                    yield half.astype(F32) * (scale * (1.0 / (STEPS * UNIT)))
            n += 1

    ids = jnp.transpose(info.astype(F32))
    block = lax.broadcasted_iota(I32, (BLOCKS, DEVICES), 0).astype(F32)
    picks = jnp.concatenate(
        [jnp.where(ids[k : k + 1] == block, 1.0, 0.0).astype(BF16) for k in range(SEL)], axis=1
    )
    values = jnp.concatenate([value for row in range(STATE_ROW) for value in decoded(row, 2 * row)], axis=0)
    ones = jnp.ones((SEL * DEVICES, BS), BF16)
    sums = jnp.dot(picks, jnp.concatenate([*three_terms(values), ones], axis=1), preferred_element_type=F32)
    totals = (sums[:, :BS] + sums[:, BS : 2 * BS]) + sums[:, 2 * BS : 3 * BS]
    tallies = sums[:, 3 * BS :]

    states = []
    for array in range(3):
        held = jnp.concatenate(list(decoded(STATE_ROW + array, SEL + OWNCAP * array)), axis=0)
        states += three_terms(held)
    found = jnp.dot(slot_map[...], jnp.concatenate(states, axis=1), preferred_element_type=F32)
    term = [found[:, n * BS : (n + 1) * BS] for n in range(9)]
    moment1, root2, master = [(term[3 * a] + term[3 * a + 1]) + term[3 * a + 2] for a in range(3)]

    direction = adamw(totals, master, moment1, root2 * root2)[2]
    direction = jnp.where(tallies > 0.5, direction, 0.0).astype(BF16)
    for i in range(PLANE):
        message[i] = direction

    padded = jnp.concatenate([totals, jnp.zeros((2 * BS - BLOCKS, BS), F32)], axis=0)
    sums = jnp.dot(block_map[...], jnp.concatenate(three_terms(padded), axis=1), preferred_element_type=F32)
    owned[...] = (sums[:, :BS] + sums[:, BS : 2 * BS]) + sums[:, 2 * BS :]

    padded = jnp.concatenate([tallies, jnp.zeros((2 * BS - BLOCKS, BS), F32)], axis=0).astype(BF16)
    flags[...] = jnp.dot(own_map[...], padded, preferred_element_type=F32)


def directions(got, slot_map, block_map, own_map):
    return pl.pallas_call(
        directions_kernel,
        in_specs=[VMEM] * 4,
        out_specs=[VMEM] * 3,
        out_shape=[
            jax.ShapeDtypeStruct((PLANE, BLOCKS, BS), BF16),
            jax.ShapeDtypeStruct((OWNCAP * DEVICES, BS), F32),
            jax.ShapeDtypeStruct((16, BS), F32),
        ],
        compiler_params=PARAMS,
        cost_estimate=pl.CostEstimate(flops=200_000_000, bytes_accessed=2_000_000, transcendentals=20_000),
        name="directions",
    )(got, slot_map, block_map, own_map)


PITCH = BLOCKS + 1


def turn_kernel(rows, out, scratch):
    for chip in range(PLANE):
        scratch[pl.ds(chip * PITCH, BLOCKS), :] = rows[chip].astype(F32)
    for b in range(BLOCKS):
        out[b] = scratch[pl.ds(b, PLANE, stride=PITCH), :].astype(BF16)


def turn(rows):
    return pl.pallas_call(
        turn_kernel,
        in_specs=[VMEM],
        out_specs=VMEM,
        out_shape=jax.ShapeDtypeStruct((BLOCKS, PLANE, BS), BF16),
        scratch_shapes=[pltpu.VMEM((PLANE * PITCH, BS), F32)],
        compiler_params=PARAMS,
        cost_estimate=pl.CostEstimate(flops=600_000, bytes_accessed=1_200_000, transcendentals=0),
        name="turn",
    )(rows)


def place(steps, pieces):
    arrays = [a for piece in pieces for a in piece[2:]]

    def kernel(*refs):
        inputs, out, sems = refs[: len(arrays)], refs[-2], refs[-1]
        z, core = lax.axis_index("z"), lax.axis_index("core")
        copies = []
        for n, ref in enumerate(inputs):
            first, away = pieces[n // 2][:2]
            at = first_row(lax.rem(z + away, N_COL // 2), core if n % 2 == 0 else 1 - core)
            target = out.at[pl.ds(first, ref.shape[0]), pl.ds(pl.multiple_of(at, PLANE), PLANE)]
            copies.append(pltpu.make_async_copy(ref, target, sems.at[n]))
        for copy in copies:
            copy.start()
        for copy in copies:
            copy.wait()

    return pl.pallas_call(
        kernel,
        in_specs=[VMEM] * len(arrays) + ([] if steps is None else [HBM]),
        out_specs=HBM,
        out_shape=jax.ShapeDtypeStruct((BLOCKS, BS, BS), BF16),
        scratch_shapes=[pltpu.SemaphoreType.DMA((len(arrays),))],
        input_output_aliases={} if steps is None else {len(arrays): 0},
        compiler_params=PARAMS,
        cost_estimate=pl.CostEstimate(flops=0, bytes_accessed=2_400_000, transcendentals=0),
        name="place",
    )(*arrays, *([] if steps is None else [steps]))


def update_kernel(owned, flags, master, moment1, moment2, master_out, moment1_out, moment2_out, totals):
    for s in range(OWNCAP):
        for col in range(N_COL):
            at = first_row(col // 2, col % 2)
            totals[s, at : at + PLANE] = owned[pl.ds(col * OWNCAP + s, PLANE, stride=N_COL * OWNCAP), :]
        changed = flags[s : s + 1] > 0.5
        new1, new2, direction = adamw(totals[s], master[s], moment1[s], moment2[s])
        master_out[s] = jnp.where(changed, master[s] - LEARN_RATE * direction, master[s])
        moment1_out[s] = jnp.where(changed, new1, moment1[s])
        moment2_out[s] = jnp.where(changed, new2, moment2[s])


def update(owned, flags, master, moment1, moment2):
    slots = jax.ShapeDtypeStruct((OWNCAP, BS, BS), F32)
    return pl.pallas_call(
        update_kernel,
        in_specs=[VMEM] * 5,
        out_specs=[VMEM] * 3,
        out_shape=[slots] * 3,
        scratch_shapes=[pltpu.VMEM((OWNCAP, BS, BS), F32)],
        compiler_params=PARAMS,
        cost_estimate=pl.CostEstimate(flops=600_000, bytes_accessed=900_000, transcendentals=33_000),
        name="update",
    )(owned, flags, master, moment1, moment2)


RIGHT = [(i, (i + 1) % 4) for i in range(4)]
LEFT = [(i, (i + 3) % 4) for i in range(4)]


def local(grad, error, sel_blocks, row_bounds, col_bounds, master, moment1, moment2):
    send = pack(sel_blocks, grad, error, master, moment1, moment2)
    got = lax.all_to_all(send, ("row", "z", "core"), split_axis=0, concat_axis=0, tiled=True)
    slot_map, block_map, own_map = maps(row_bounds, col_bounds)
    error_out = feedback(sel_blocks, grad, error, 0, None)
    got, error_out = lax.optimization_barrier((got, error_out))
    message, owned, flags = directions(got, slot_map, block_map, own_map)

    message, error_out = lax.optimization_barrier((message, error_out))
    plane = lax.all_to_all(message.reshape(PLANE * BLOCKS, BS), "row", split_axis=0, concat_axis=0, tiled=True)
    error_out = feedback(sel_blocks, grad, error, 1, error_out)
    plane, error_out = lax.optimization_barrier((plane, error_out))
    mine = turn(plane.reshape(PLANE, BLOCKS, BS))
    mine, owned = lax.optimization_barrier((mine, owned))

    def swap(piece):
        return lax.ppermute(piece, "core", [(0, 1), (1, 0)])

    half = BLOCKS // 2
    before = lax.ppermute(mine, "z", RIGHT)
    after = lax.ppermute(mine, "z", LEFT)
    mine_too = swap(mine)
    owned = lax.all_to_all(owned, ("row", "z", "core"), split_axis=0, concat_axis=0, tiled=True)
    before, after, mine_too, owned = lax.optimization_barrier((before, after, mine_too, owned))
    far_first = lax.ppermute(before[:half], "z", RIGHT)
    far_last = lax.ppermute(after[half:], "z", LEFT)
    steps = place(None, [(0, 0, mine, mine_too), (0, 3, before, swap(before)), (0, 1, after, swap(after))])
    states = update(owned, flags, master, moment1, moment2)
    far_first, far_last, steps, states = lax.optimization_barrier((far_first, far_last, steps, states))
    steps = place(steps, [(0, 2, far_first, swap(far_first)), (half, 2, far_last, swap(far_last))])
    return (error_out, *states, steps)


def solution(mesh):
    cores = Mesh(mesh.devices.reshape(N_ROW, N_COL // 2, 2), ("row", "z", "core"))
    split = P(("row", "z", "core"))
    return jax.shard_map(
        local,
        mesh=cores,
        in_specs=(split, split, split, P(), P(), split, split, split),
        out_specs=(split, split, split, split, P()),
        check_vma=False,
    )
```

```python
import jax
import jax.numpy as jnp
from jax import lax
from jax.experimental import pallas as pl
from jax.experimental.pallas import tpu as pltpu
from jax.sharding import Mesh
from jax.sharding import PartitionSpec as P

BS = 128
GC = 6
GR = 24
BLOCKS = 144
SEL = 7
OWNCAP = 2
N_ROW = 16
N_COL = 8
DEVICES = N_ROW * N_COL
PLANE = N_ROW
CHIPS = 4 * PLANE
HALF = BS // 2

MSG = 8
STATE_ROW = 4
INFO_ROW = 7
SCALE_LANE = 8
EXT = 8
UNIT = 2.0**26
STEPS = 32767.0
ROOT_STEPS = 65535.0
ROOT_LOW = 32768.0

BETA_ONE = 0.9
BETA_TWO = 0.95
EPSILON = 1e-08
DECAY_RATE = 0.1
LEARN_RATE = 0.01
CORRECT_ONE = 1.0 - 0.9**10
CORRECT_TWO = 1.0 - 0.95**10

F32 = jnp.float32
BF16 = jnp.bfloat16
I32 = jnp.int32
SMEM = pl.BlockSpec(memory_space=pltpu.SMEM)
VMEM = pl.BlockSpec(memory_space=pltpu.VMEM)
HBM = pl.BlockSpec(memory_space=pltpu.HBM)
ANY = pl.BlockSpec(memory_space=pl.ANY)
MIB = 1024 * 1024
PARAMS = pltpu.CompilerParams(vmem_limit_bytes=16 * MIB)
ALONE = pltpu.CompilerParams(vmem_limit_bytes=64 * MIB)


def adamw(totals, master, moment1, moment2):
    averaged = totals / DEVICES
    first = BETA_ONE * moment1 + (1.0 - BETA_ONE) * averaged
    second = BETA_TWO * moment2 + (1.0 - BETA_TWO) * averaged * averaged
    direction = first / CORRECT_ONE / (jnp.sqrt(second / CORRECT_TWO) + EPSILON) + DECAY_RATE * master
    return first, second, direction


def three_terms(x):
    high = x.astype(BF16)
    rest = x - high.astype(F32)
    middle = rest.astype(BF16)
    low = (rest - middle.astype(F32)).astype(BF16)
    return high, middle, low


def first_row(z, core):
    return core * HALF + z * PLANE


def pack_kernel(sel_hbm, grad, error, master, moment1, moment2, send, sel, grads, errors, states, sel_sem, sems):
    fetch_sel = pltpu.make_async_copy(sel_hbm, sel, sel_sem)
    fetch_sel.start()
    held = [
        pltpu.make_async_copy(array, states.at[n], sems.at[2 * SEL + n])
        for n, array in enumerate((moment1, moment2, master))
    ]
    for copy in held:
        copy.start()
    fetch_sel.wait()
    chosen = []
    for k in range(SEL):
        at = jnp.minimum(sel[0, k], BLOCKS - 1)
        chosen.append(pltpu.make_async_copy(grad.at[at], grads.at[k], sems.at[k]))
        chosen.append(pltpu.make_async_copy(error.at[at], errors.at[k], sems.at[SEL + k]))
    for copy in chosen:
        copy.start()

    def put(row, block):
        for col in range(N_COL):
            at = first_row(col // 2, col % 2)
            send[pl.ds(col * MSG + row, PLANE, stride=N_COL * MSG), :] = block[at : at + PLANE]

    lane = lax.broadcasted_iota(I32, (BS, BS), 1)
    info = jnp.zeros((BS, BS), I32)
    for k in range(SEL):
        info = jnp.where(lane == k, sel[0, k], info)

    def coded(n, info, block, root=False):
        scale = jnp.maximum(jnp.ceil(jnp.max(jnp.abs(block), axis=1, keepdims=True) * UNIT), 1.0)
        info = jnp.where(lane == SCALE_LANE + n, scale.astype(I32), info)
        if root:
            return jnp.round(block * (ROOT_STEPS * UNIT / scale) - ROOT_LOW).astype(I32), info
        return jnp.round(block * (STEPS * UNIT / scale)).astype(I32), info

    def put_pair(row, first, second):
        put(row, lax.shift_left(first, 16) | (second & 0xFFFF))

    for n in range(3):
        held[n].wait()
        pair = []
        for s in range(OWNCAP):
            block = states[n, s]
            code, info = coded(SEL + OWNCAP * n + s, info, jnp.sqrt(block) if n == 1 else block, n == 1)
            pair.append(code)
        put_pair(STATE_ROW + n, *pair)
    pair = []
    for k in range(SEL):
        chosen[2 * k].wait()
        chosen[2 * k + 1].wait()
        code, info = coded(k, info, grads[k].astype(F32) + errors[k])
        pair.append(code)
        if len(pair) == 2:
            put_pair(k // 2, *pair)
            pair = []
    put_pair(SEL // 2, pair[0], jnp.zeros((BS, BS), I32))
    put(INFO_ROW, info)


def pack(sel, grad, error, master, moment1, moment2):
    return pl.pallas_call(
        pack_kernel,
        in_specs=[HBM] * 6,
        out_specs=VMEM,
        out_shape=jax.ShapeDtypeStruct((DEVICES * MSG, BS), I32),
        scratch_shapes=[
            pltpu.SMEM((1, SEL), I32),
            pltpu.VMEM((SEL, BS, BS), BF16),
            pltpu.VMEM((SEL, BS, BS), F32),
            pltpu.VMEM((3, OWNCAP, BS, BS), F32),
            pltpu.SemaphoreType.DMA,
            pltpu.SemaphoreType.DMA((2 * SEL + 3,)),
        ],
        compiler_params=ALONE,
        cost_estimate=pl.CostEstimate(flops=200_000, bytes_accessed=2_200_000, transcendentals=0),
        name="pack_rows",
    )(sel, grad, error, master, moment1, moment2)


def band(cuts, bands, positions):
    index = jnp.zeros_like(positions)
    start = jnp.zeros_like(positions)
    for k in range(1, bands):
        past = cuts[k] <= positions
        index = index + past.astype(I32)
        start = jnp.where(past, cuts[k], start)
    return index, start


FEED = 18


def feedback_kernel(sel, grad, error, out):
    def step(grad_blocks, error_blocks, out_blocks):
        first = pl.program_id(0) * FEED
        for b in range(FEED):
            hit = sel[0, 0] == first + b
            for k in range(1, SEL):
                hit = jnp.logical_or(hit, sel[0, k] == first + b)
            keep = 1.0 - hit.astype(F32)
            out_blocks[b] = (grad_blocks[b].astype(F32) + error_blocks[b]) * keep

    block = pl.BlockSpec((FEED, BS, BS), lambda i: (i, 0, 0))
    pltpu.emit_pipeline(step, grid=(BLOCKS // FEED,), in_specs=[block, block], out_specs=[block])(grad, error, out)


def feedback(sel, grad, error):
    return pl.pallas_call(
        feedback_kernel,
        in_specs=[SMEM] + [HBM] * 2,
        out_specs=HBM,
        out_shape=jax.ShapeDtypeStruct((BLOCKS, BS, BS), F32),
        compiler_params=PARAMS,
        cost_estimate=pl.CostEstimate(flops=5_000_000, bytes_accessed=23_600_000, transcendentals=0),
        name="error_feedback",
    )(sel, grad, error)


def maps_kernel(rows_ref, cols_ref, slot_map, block_map, own_map):
    block = lax.broadcasted_iota(I32, (BLOCKS, BS), 0)
    lane = lax.broadcasted_iota(I32, (BLOCKS, BS), 1)
    grid_row = block // GC
    grid_col = block - grid_row * GC
    row_band, row_start = band(rows_ref, N_ROW, grid_row)
    col_band, col_start = band(cols_ref, N_COL, grid_col)
    owner = row_band * N_COL + col_band
    slot = (grid_row - row_start) + (grid_col - col_start)
    for s in range(OWNCAP):
        slot_map[:, s * BS : (s + 1) * BS] = jnp.where((owner == lane) & (slot == s), 1.0, 0.0).astype(BF16)
    holder = lax.broadcasted_iota(I32, (EXT * CHIPS, BS), 0)
    chip = holder // EXT
    slot = holder % OWNCAP
    core = lax.axis_index("core")
    band_row = chip // 4
    band_col = chip % 4 * 2 + jnp.where(holder % 4 < OWNCAP, core, 1 - core)
    top = jnp.zeros_like(holder)
    end = jnp.zeros_like(holder)
    for k in range(N_ROW):
        top = jnp.where(band_row == k, rows_ref[k], top)
        end = jnp.where(band_row == k, rows_ref[k + 1], end)
    left = jnp.zeros_like(holder)
    right = jnp.zeros_like(holder)
    for k in range(N_COL):
        left = jnp.where(band_col == k, cols_ref[k], left)
        right = jnp.where(band_col == k, cols_ref[k + 1], right)
    at_row = top + slot
    target = jnp.where((at_row < end) & (left < right), at_row * GC + left, -1)
    lane = lax.broadcasted_iota(I32, (EXT * CHIPS, BS), 1)
    for part in range(2):
        block_map[:, part * BS : (part + 1) * BS] = jnp.where(target == lane + part * BS, 1.0, 0.0).astype(BF16)
    band_row = lax.axis_index("row")
    band_col = 2 * lax.axis_index("z") + lax.axis_index("core")
    slot = lax.broadcasted_iota(I32, (16, 2 * BS), 0)
    at_row = rows_ref[band_row] + slot
    left = cols_ref[band_col]
    inside = (slot < OWNCAP) & (at_row < rows_ref[band_row + 1]) & (left < cols_ref[band_col + 1])
    lane = lax.broadcasted_iota(I32, (16, 2 * BS), 1)
    own_map[...] = jnp.where(inside & (at_row * GC + left == lane), 1.0, 0.0).astype(BF16)


def maps(row_bounds, col_bounds):
    return pl.pallas_call(
        maps_kernel,
        in_specs=[SMEM] * 2,
        out_specs=[VMEM] * 3,
        out_shape=[
            jax.ShapeDtypeStruct((BLOCKS, OWNCAP * BS), BF16),
            jax.ShapeDtypeStruct((EXT * CHIPS, 2 * BS), BF16),
            jax.ShapeDtypeStruct((16, 2 * BS), BF16),
        ],
        compiler_params=PARAMS,
        cost_estimate=pl.CostEstimate(flops=500_000, bytes_accessed=300_000, transcendentals=0),
        name="slot_maps",
    )(row_bounds, col_bounds)


def directions_kernel(got, slot_map, block_map, own_map, message, flags):
    def rows(k):
        return got[pl.ds(k, DEVICES, stride=MSG), :]

    info = rows(INFO_ROW)

    def decoded(row, n):
        words = rows(row)
        for half in (lax.shift_right_arithmetic(words, 16), lax.shift_right_arithmetic(lax.shift_left(words, 16), 16)):
            if n < SEL or row > SEL // 2:
                scale = info[:, SCALE_LANE + n : SCALE_LANE + n + 1].astype(F32)
                if row == STATE_ROW + 1:
                    yield (half.astype(F32) + ROOT_LOW) * (scale * (1.0 / (ROOT_STEPS * UNIT)))
                else:
                    yield half.astype(F32) * (scale * (1.0 / (STEPS * UNIT)))
            n += 1

    ids = jnp.transpose(info.astype(F32))
    block = lax.broadcasted_iota(I32, (BLOCKS, DEVICES), 0).astype(F32)
    picks = jnp.concatenate(
        [jnp.where(ids[k : k + 1] == block, 1.0, 0.0).astype(BF16) for k in range(SEL)], axis=1
    )
    values = jnp.concatenate([value for row in range(STATE_ROW) for value in decoded(row, 2 * row)], axis=0)
    ones = jnp.ones((SEL * DEVICES, BS), BF16)
    sums = jnp.dot(picks, jnp.concatenate([*three_terms(values), ones], axis=1), preferred_element_type=F32)
    totals = (sums[:, :BS] + sums[:, BS : 2 * BS]) + sums[:, 2 * BS : 3 * BS]
    tallies = sums[:, 3 * BS :]

    states = []
    for array in range(3):
        held = jnp.concatenate(list(decoded(STATE_ROW + array, SEL + OWNCAP * array)), axis=0)
        states += three_terms(held)
    found = jnp.dot(slot_map[...], jnp.concatenate(states, axis=1), preferred_element_type=F32)
    term = [found[:, n * BS : (n + 1) * BS] for n in range(9)]
    moment1, root2, master = [(term[3 * a] + term[3 * a + 1]) + term[3 * a + 2] for a in range(3)]

    direction = adamw(totals, master, moment1, root2 * root2)[2]
    direction = jnp.where(tallies > 0.5, direction, 0.0).astype(BF16)
    padded = jnp.concatenate([totals, jnp.zeros((2 * BS - BLOCKS, BS), F32)], axis=0)
    sums = jnp.dot(block_map[...], jnp.concatenate(three_terms(padded), axis=1), preferred_element_type=F32)
    high, low, _ = three_terms((sums[:, :BS] + sums[:, BS : 2 * BS]) + sums[:, 2 * BS :])
    term = lax.broadcasted_iota(I32, (EXT * CHIPS, BS), 0) % EXT < EXT // 2
    both = jnp.where(term, high.astype(F32), low.astype(F32)).astype(BF16).reshape(CHIPS, EXT, BS)
    for i in range(CHIPS):
        message[i, :BLOCKS] = direction
        message[i, BLOCKS:] = both[i]

    padded = jnp.concatenate([tallies, jnp.zeros((2 * BS - BLOCKS, BS), F32)], axis=0).astype(BF16)
    flags[...] = jnp.dot(own_map[...], padded, preferred_element_type=F32)


def directions(got, slot_map, block_map, own_map):
    return pl.pallas_call(
        directions_kernel,
        in_specs=[VMEM] * 4,
        out_specs=[VMEM] * 2,
        out_shape=[
            jax.ShapeDtypeStruct((CHIPS, BLOCKS + EXT, BS), BF16),
            jax.ShapeDtypeStruct((16, BS), F32),
        ],
        compiler_params=PARAMS,
        cost_estimate=pl.CostEstimate(flops=200_000_000, bytes_accessed=2_000_000, transcendentals=20_000),
        name="directions",
    )(got, slot_map, block_map, own_map)


PITCH = BLOCKS + 1


EXT_PITCH = EXT + 1


def turn_kernel(rows, first, last, own, other, scratch, ext):
    for z in range(4):
        for y in range(PLANE):
            chip = 4 * y + z
            scratch[pl.ds(y * PITCH, BLOCKS), :] = rows[chip, :BLOCKS].astype(F32)
            ext[pl.ds((z * PLANE + y) * EXT_PITCH, EXT), :] = rows[chip, BLOCKS:].astype(F32)
        for b in range(BLOCKS):
            (first, last)[z // 2][z % 2, b] = scratch[pl.ds(b, PLANE, stride=PITCH), :].astype(BF16)
    for t in range(2 * OWNCAP):
        high, low = [ext[pl.ds(t + 4 * n, CHIPS, stride=EXT_PITCH), :] for n in range(2)]
        (own, other)[t // OWNCAP][t % OWNCAP] = high + low


def turn(rows):
    planes = jax.ShapeDtypeStruct((2, BLOCKS, PLANE, BS), BF16)
    owned = jax.ShapeDtypeStruct((OWNCAP, HALF, BS), F32)
    return pl.pallas_call(
        turn_kernel,
        in_specs=[VMEM],
        out_specs=[VMEM] * 4,
        out_shape=[planes, planes, owned, owned],
        scratch_shapes=[pltpu.VMEM((PLANE * PITCH, BS), F32), pltpu.VMEM((CHIPS * EXT_PITCH, BS), F32)],
        compiler_params=PARAMS,
        cost_estimate=pl.CostEstimate(flops=2_400_000, bytes_accessed=5_000_000, transcendentals=0),
        name="turn",
    )(rows)


def place(pieces, steps, sems, half):
    copies = []
    for first, planes in pieces:
        for z in range(first, first + 2):
            rows = pl.ds(pl.multiple_of(first_row(z, half), PLANE), PLANE)
            copies.append(pltpu.make_async_copy(planes.at[z - first], steps.at[:, rows], sems.at[z]))
            copies[-1].start()
    return copies


def place_own(first, last):
    def kernel(first, last, steps, sems):
        for copy in place([(0, first), (2, last)], steps, sems, lax.axis_index("core")):
            copy.wait()

    return pl.pallas_call(
        kernel,
        in_specs=[VMEM] * 2,
        out_specs=HBM,
        out_shape=jax.ShapeDtypeStruct((BLOCKS, BS, BS), BF16),
        scratch_shapes=[pltpu.SemaphoreType.DMA((4,))],
        compiler_params=PARAMS,
        cost_estimate=pl.CostEstimate(flops=0, bytes_accessed=4_800_000, transcendentals=0),
        name="place_own",
    )(first, last)


def place_first(planes, steps):
    def kernel(planes, before, steps, sems):
        for copy in place([(0, planes)], steps, sems, 1 - lax.axis_index("core")):
            copy.wait()

    return pl.pallas_call(
        kernel,
        in_specs=[VMEM, HBM],
        out_specs=HBM,
        out_shape=jax.ShapeDtypeStruct((BLOCKS, BS, BS), BF16),
        scratch_shapes=[pltpu.SemaphoreType.DMA((4,))],
        input_output_aliases={1: 0},
        compiler_params=PARAMS,
        cost_estimate=pl.CostEstimate(flops=0, bytes_accessed=2_400_000, transcendentals=0),
        name="place_first",
    )(planes, steps)


def finish_kernel(
    planes, before, own, other, flags, master, moment1, moment2, steps, master_out, moment1_out, moment2_out,
    totals, new, sems, new_sems,
):
    core = lax.axis_index("core")
    copies = place([(2, planes)], steps, sems, 1 - core)
    totals[:, pl.ds(pl.multiple_of(core * HALF, HALF), HALF), :] = own[...]
    totals[:, pl.ds(pl.multiple_of((1 - core) * HALF, HALF), HALF), :] = other[...]
    for s in range(OWNCAP):
        changed = flags[s : s + 1] > 0.5
        new1, new2, direction = adamw(totals[s], master[s], moment1[s], moment2[s])
        new[0, s] = jnp.where(changed, master[s] - LEARN_RATE * direction, master[s])
        new[1, s] = jnp.where(changed, new1, moment1[s])
        new[2, s] = jnp.where(changed, new2, moment2[s])
        for n, array in enumerate((master_out, moment1_out, moment2_out)):
            copies.append(pltpu.make_async_copy(new.at[n, s], array.at[s], new_sems.at[n, s]))
            copies[-1].start()
    for copy in copies:
        copy.wait()


def finish(planes, steps, own, other, flags, master, moment1, moment2):
    slots = jax.ShapeDtypeStruct((OWNCAP, BS, BS), F32)
    return pl.pallas_call(
        finish_kernel,
        in_specs=[VMEM, HBM] + [VMEM] * 6,
        out_specs=[HBM] * 4,
        out_shape=[jax.ShapeDtypeStruct((BLOCKS, BS, BS), BF16), slots, slots, slots],
        scratch_shapes=[
            pltpu.VMEM((OWNCAP, BS, BS), F32),
            pltpu.VMEM((3, OWNCAP, BS, BS), F32),
            pltpu.SemaphoreType.DMA((4,)),
            pltpu.SemaphoreType.DMA((3, OWNCAP)),
        ],
        input_output_aliases={1: 0},
        compiler_params=PARAMS,
        cost_estimate=pl.CostEstimate(flops=600_000, bytes_accessed=3_600_000, transcendentals=33_000),
        name="finish",
    )(planes, steps, own, other, flags, master, moment1, moment2)


def swap(piece):
    return lax.ppermute(piece, "core", [(0, 1), (1, 0)])


def local(grad, error, sel_blocks, row_bounds, col_bounds, master, moment1, moment2):
    send = pack(sel_blocks, grad, error, master, moment1, moment2)
    got = lax.all_to_all(send, ("row", "z", "core"), split_axis=0, concat_axis=0, tiled=True)
    slot_map, block_map, own_map = maps(row_bounds, col_bounds)
    message, flags = directions(got, slot_map, block_map, own_map)
    rows = BLOCKS + EXT
    chips = lax.all_to_all(message.reshape(CHIPS * rows, BS), ("row", "z"), split_axis=0, concat_axis=0, tiled=True)
    error_out = feedback(sel_blocks, grad, error)
    chips, error_out = lax.optimization_barrier((chips, error_out))
    first, last, own, other = turn(chips.reshape(CHIPS, rows, BS))
    first_too, last_too, other = swap(first), swap(last), swap(other)
    steps = place_own(first, last)
    first_too, steps = lax.optimization_barrier((first_too, steps))
    steps = place_first(first_too, steps)
    steps, *states = finish(last_too, steps, own, other, flags, master, moment1, moment2)
    return (error_out, *states, steps)


def solution(mesh):
    cores = Mesh(mesh.devices.reshape(N_ROW, N_COL // 2, 2), ("row", "z", "core"))
    split = P(("row", "z", "core"))
    return jax.shard_map(
        local,
        mesh=cores,
        in_specs=(split, split, split, P(), P(), split, split, split),
        out_specs=(split, split, split, split, P()),
        check_vma=False,
    )
```

```python
import jax
import jax.numpy as jnp
from jax import lax
from jax.experimental import pallas as pl
from jax.experimental.pallas import tpu as pltpu
from jax.sharding import Mesh
from jax.sharding import PartitionSpec as P

BS = 128
GC = 6
GR = 24
BLOCKS = 144
SEL = 7
OWNCAP = 2
N_ROW = 16
N_COL = 8
DEVICES = N_ROW * N_COL
PLANE = N_ROW
CHIPS = 4 * PLANE

MSG = 8
STATE_ROW = 4
INFO_ROW = 7
SCALE_LANE = 8
RIDE = 8
UNIT = 2.0**26
STEPS = 32767.0
ROOT_STEPS = 65535.0
ROOT_LOW = 32768.0

BETA_ONE = 0.9
BETA_TWO = 0.95
EPSILON = 1e-08
DECAY_RATE = 0.1
LEARN_RATE = 0.01
CORRECT_ONE = 1.0 - 0.9**10
CORRECT_TWO = 1.0 - 0.95**10

F32 = jnp.float32
BF16 = jnp.bfloat16
I32 = jnp.int32
SMEM = pl.BlockSpec(memory_space=pltpu.SMEM)
VMEM = pl.BlockSpec(memory_space=pltpu.VMEM)
HBM = pl.BlockSpec(memory_space=pltpu.HBM)
ANY = pl.BlockSpec(memory_space=pl.ANY)
MIB = 1024 * 1024
PARAMS = pltpu.CompilerParams(vmem_limit_bytes=16 * MIB)
ALONE = pltpu.CompilerParams(vmem_limit_bytes=64 * MIB)
NEARLY_ALONE = pltpu.CompilerParams(vmem_limit_bytes=61 * MIB)


def adamw(totals, master, moment1, moment2):
    averaged = totals / DEVICES
    first = BETA_ONE * moment1 + (1.0 - BETA_ONE) * averaged
    second = BETA_TWO * moment2 + (1.0 - BETA_TWO) * averaged * averaged
    direction = first / CORRECT_ONE / (jnp.sqrt(second / CORRECT_TWO) + EPSILON) + DECAY_RATE * master
    return first, second, direction


def three_terms(x):
    high = x.astype(BF16)
    rest = x - high.astype(F32)
    middle = rest.astype(BF16)
    low = (rest - middle.astype(F32)).astype(BF16)
    return high, middle, low


def first_row(z, core):
    return core * (BS // 2) + z * PLANE


def pack_kernel(sel_hbm, grad, error, master, moment1, moment2, send, sel, grads, errors, states, sel_sem, sems):
    fetch_sel = pltpu.make_async_copy(sel_hbm, sel, sel_sem)
    fetch_sel.start()
    held = [
        pltpu.make_async_copy(array, states.at[n], sems.at[2 * SEL + n])
        for n, array in enumerate((moment1, moment2, master))
    ]
    for copy in held:
        copy.start()
    fetch_sel.wait()
    chosen = []
    for k in range(SEL):
        at = jnp.minimum(sel[0, k], BLOCKS - 1)
        chosen.append(pltpu.make_async_copy(grad.at[at], grads.at[k], sems.at[k]))
        chosen.append(pltpu.make_async_copy(error.at[at], errors.at[k], sems.at[SEL + k]))
    for copy in chosen:
        copy.start()

    def put(row, block):
        for col in range(N_COL):
            at = first_row(col // 2, col % 2)
            send[pl.ds(col * MSG + row, PLANE, stride=N_COL * MSG), :] = block[at : at + PLANE]

    lane = lax.broadcasted_iota(I32, (BS, BS), 1)
    info = jnp.zeros((BS, BS), I32)
    for k in range(SEL):
        info = jnp.where(lane == k, sel[0, k], info)

    def coded(n, info, block, root=False):
        scale = jnp.maximum(jnp.ceil(jnp.max(jnp.abs(block), axis=1, keepdims=True) * UNIT), 1.0)
        info = jnp.where(lane == SCALE_LANE + n, scale.astype(I32), info)
        if root:
            return jnp.round(block * (ROOT_STEPS * UNIT / scale) - ROOT_LOW).astype(I32), info
        return jnp.round(block * (STEPS * UNIT / scale)).astype(I32), info

    def put_pair(row, first, second):
        put(row, lax.shift_left(first, 16) | (second & 0xFFFF))

    for n in range(3):
        held[n].wait()
        pair = []
        for s in range(OWNCAP):
            block = states[n, s]
            code, info = coded(SEL + OWNCAP * n + s, info, jnp.sqrt(block) if n == 1 else block, n == 1)
            pair.append(code)
        put_pair(STATE_ROW + n, *pair)
    pair = []
    for k in range(SEL):
        chosen[2 * k].wait()
        chosen[2 * k + 1].wait()
        code, info = coded(k, info, grads[k].astype(F32) + errors[k])
        pair.append(code)
        if len(pair) == 2:
            put_pair(k // 2, *pair)
            pair = []
    put_pair(SEL // 2, pair[0], jnp.zeros((BS, BS), I32))
    put(INFO_ROW, info)


def pack(sel, grad, error, master, moment1, moment2):
    return pl.pallas_call(
        pack_kernel,
        in_specs=[HBM] * 6,
        out_specs=VMEM,
        out_shape=jax.ShapeDtypeStruct((DEVICES * MSG, BS), I32),
        scratch_shapes=[
            pltpu.SMEM((1, SEL), I32),
            pltpu.VMEM((SEL, BS, BS), BF16),
            pltpu.VMEM((SEL, BS, BS), F32),
            pltpu.VMEM((3, OWNCAP, BS, BS), F32),
            pltpu.SemaphoreType.DMA,
            pltpu.SemaphoreType.DMA((2 * SEL + 3,)),
        ],
        compiler_params=ALONE,
        cost_estimate=pl.CostEstimate(flops=200_000, bytes_accessed=2_200_000, transcendentals=0),
        name="pack_rows",
    )(sel, grad, error, master, moment1, moment2)


def band(cuts, bands, positions):
    index = jnp.zeros_like(positions)
    start = jnp.zeros_like(positions)
    for k in range(1, bands):
        past = cuts[k] <= positions
        index = index + past.astype(I32)
        start = jnp.where(past, cuts[k], start)
    return index, start


FEED = 18


def feedback(sel, grad, error, part, before):
    steps = BLOCKS // FEED // 2

    def kernel(*refs):
        sel, grad, error, out = *refs[:3], refs[-1]

        def step(grad_blocks, error_blocks, out_blocks):
            first = (part * steps + pl.program_id(0)) * FEED
            for b in range(FEED):
                hit = sel[0, 0] == first + b
                for k in range(1, SEL):
                    hit = jnp.logical_or(hit, sel[0, k] == first + b)
                keep = 1.0 - hit.astype(F32)
                out_blocks[b] = (grad_blocks[b].astype(F32) + error_blocks[b]) * keep

        block = pl.BlockSpec((FEED, BS, BS), lambda i: (part * steps + i, 0, 0))
        pltpu.emit_pipeline(step, grid=(steps,), in_specs=[block, block], out_specs=[block])(grad, error, out)

    more = [] if before is None else [before]
    return pl.pallas_call(
        kernel,
        in_specs=[SMEM] + [HBM] * 2 + [HBM] * len(more),
        out_specs=HBM,
        out_shape=jax.ShapeDtypeStruct((BLOCKS, BS, BS), F32),
        input_output_aliases={3: 0} if more else {},
        compiler_params=NEARLY_ALONE,
        cost_estimate=pl.CostEstimate(flops=2_500_000, bytes_accessed=11_800_000, transcendentals=0),
        name="error_feedback",
    )(sel, grad, error, *more)


def maps_kernel(rows_ref, cols_ref, slot_map, block_map, own_map):
    block = lax.broadcasted_iota(I32, (BLOCKS, BS), 0)
    lane = lax.broadcasted_iota(I32, (BLOCKS, BS), 1)
    grid_row = block // GC
    grid_col = block - grid_row * GC
    row_band, row_start = band(rows_ref, N_ROW, grid_row)
    col_band, col_start = band(cols_ref, N_COL, grid_col)
    owner = row_band * N_COL + col_band
    slot = (grid_row - row_start) + (grid_col - col_start)
    for s in range(OWNCAP):
        slot_map[:, s * BS : (s + 1) * BS] = jnp.where((owner == lane) & (slot == s), 1.0, 0.0).astype(BF16)
    holder = lax.broadcasted_iota(I32, (RIDE * CHIPS, BS), 0)
    chip = holder // RIDE
    slot = holder % OWNCAP
    core = lax.axis_index("core")
    band_row = chip % PLANE
    at_z = lax.axis_index("z") + chip // PLANE
    at_z = jnp.where(at_z >= 4, at_z - 4, at_z)
    band_col = at_z * 2 + jnp.where(holder % 4 < OWNCAP, core, 1 - core)
    top = jnp.zeros_like(holder)
    end = jnp.zeros_like(holder)
    for k in range(N_ROW):
        top = jnp.where(band_row == k, rows_ref[k], top)
        end = jnp.where(band_row == k, rows_ref[k + 1], end)
    left = jnp.zeros_like(holder)
    right = jnp.zeros_like(holder)
    for k in range(N_COL):
        left = jnp.where(band_col == k, cols_ref[k], left)
        right = jnp.where(band_col == k, cols_ref[k + 1], right)
    at_row = top + slot
    target = jnp.where((at_row < end) & (left < right), at_row * GC + left, -1)
    lane = lax.broadcasted_iota(I32, (RIDE * CHIPS, BS), 1)
    for part in range(2):
        block_map[:, part * BS : (part + 1) * BS] = jnp.where(target == lane + part * BS, 1.0, 0.0).astype(BF16)
    band_row = lax.axis_index("row")
    band_col = 2 * lax.axis_index("z") + lax.axis_index("core")
    slot = lax.broadcasted_iota(I32, (16, 2 * BS), 0)
    at_row = rows_ref[band_row] + slot
    left = cols_ref[band_col]
    inside = (slot < OWNCAP) & (at_row < rows_ref[band_row + 1]) & (left < cols_ref[band_col + 1])
    lane = lax.broadcasted_iota(I32, (16, 2 * BS), 1)
    own_map[...] = jnp.where(inside & (at_row * GC + left == lane), 1.0, 0.0).astype(BF16)


def maps(row_bounds, col_bounds):
    return pl.pallas_call(
        maps_kernel,
        in_specs=[SMEM] * 2,
        out_specs=[VMEM] * 3,
        out_shape=[
            jax.ShapeDtypeStruct((BLOCKS, OWNCAP * BS), BF16),
            jax.ShapeDtypeStruct((RIDE * CHIPS, 2 * BS), BF16),
            jax.ShapeDtypeStruct((16, 2 * BS), BF16),
        ],
        compiler_params=PARAMS,
        cost_estimate=pl.CostEstimate(flops=500_000, bytes_accessed=300_000, transcendentals=0),
        name="slot_maps",
    )(row_bounds, col_bounds)


def directions_kernel(got, slot_map, block_map, own_map, message, across, flags):
    def rows(k):
        return got[pl.ds(k, DEVICES, stride=MSG), :]

    info = rows(INFO_ROW)

    def decoded(row, n):
        words = rows(row)
        for half in (lax.shift_right_arithmetic(words, 16), lax.shift_right_arithmetic(lax.shift_left(words, 16), 16)):
            if n < SEL or row > SEL // 2:
                scale = info[:, SCALE_LANE + n : SCALE_LANE + n + 1].astype(F32)
                if row == STATE_ROW + 1:
                    yield (half.astype(F32) + ROOT_LOW) * (scale * (1.0 / (ROOT_STEPS * UNIT)))
                else:
                    yield half.astype(F32) * (scale * (1.0 / (STEPS * UNIT)))
            n += 1

    ids = jnp.transpose(info.astype(F32))
    block = lax.broadcasted_iota(I32, (BLOCKS, DEVICES), 0).astype(F32)
    picks = jnp.concatenate(
        [jnp.where(ids[k : k + 1] == block, 1.0, 0.0).astype(BF16) for k in range(SEL)], axis=1
    )
    values = jnp.concatenate([value for row in range(STATE_ROW) for value in decoded(row, 2 * row)], axis=0)
    ones = jnp.ones((SEL * DEVICES, BS), BF16)
    sums = jnp.dot(picks, jnp.concatenate([*three_terms(values), ones], axis=1), preferred_element_type=F32)
    totals = (sums[:, :BS] + sums[:, BS : 2 * BS]) + sums[:, 2 * BS : 3 * BS]
    tallies = sums[:, 3 * BS :]

    states = []
    for array in range(3):
        held = jnp.concatenate(list(decoded(STATE_ROW + array, SEL + OWNCAP * array)), axis=0)
        states += three_terms(held)
    found = jnp.dot(slot_map[...], jnp.concatenate(states, axis=1), preferred_element_type=F32)
    term = [found[:, n * BS : (n + 1) * BS] for n in range(9)]
    moment1, root2, master = [(term[3 * a] + term[3 * a + 1]) + term[3 * a + 2] for a in range(3)]

    direction = adamw(totals, master, moment1, root2 * root2)[2]
    direction = jnp.where(tallies > 0.5, direction, 0.0).astype(BF16)
    padded = jnp.concatenate([totals, jnp.zeros((2 * BS - BLOCKS, BS), F32)], axis=0)
    sums = jnp.dot(block_map[...], jnp.concatenate(three_terms(padded), axis=1), preferred_element_type=F32)
    high, low, _ = three_terms((sums[:, :BS] + sums[:, BS : 2 * BS]) + sums[:, 2 * BS :])
    term = lax.broadcasted_iota(I32, (RIDE * CHIPS, BS), 0) % RIDE < RIDE // 2
    both = jnp.where(term, high.astype(F32), low.astype(F32)).astype(BF16)
    for i in range(PLANE):
        message[i, :BLOCKS] = direction
        for n, away in enumerate((0, 1, 3)):
            first = (away * PLANE + i) * RIDE
            message[i, BLOCKS + n * RIDE : BLOCKS + (n + 1) * RIDE] = both[first : first + RIDE]
    across[:BLOCKS] = direction
    across[BLOCKS:] = both[2 * PLANE * RIDE : 3 * PLANE * RIDE]

    padded = jnp.concatenate([tallies, jnp.zeros((2 * BS - BLOCKS, BS), F32)], axis=0).astype(BF16)
    flags[...] = jnp.dot(own_map[...], padded, preferred_element_type=F32)


def directions(got, slot_map, block_map, own_map):
    return pl.pallas_call(
        directions_kernel,
        in_specs=[VMEM] * 4,
        out_specs=[VMEM] * 3,
        out_shape=[
            jax.ShapeDtypeStruct((PLANE, BLOCKS + 3 * RIDE, BS), BF16),
            jax.ShapeDtypeStruct((BLOCKS + PLANE * RIDE, BS), BF16),
            jax.ShapeDtypeStruct((16, BS), F32),
        ],
        compiler_params=PARAMS,
        cost_estimate=pl.CostEstimate(flops=200_000_000, bytes_accessed=2_000_000, transcendentals=20_000),
        name="directions",
    )(got, slot_map, block_map, own_map)


PITCH = BLOCKS + 1


PIECE = BLOCKS + RIDE


def turn(rows):
    count = (rows.shape[1] - BLOCKS) // RIDE
    pitch = rows.shape[1] + 1

    def kernel(rows, *rest):
        pieces, scratch = rest[:-1], rest[-1]
        for chip in range(PLANE):
            scratch[pl.ds(chip * pitch, pitch - 1), :] = rows[chip].astype(F32)

        def tile(row):
            return scratch[pl.ds(row, PLANE, stride=pitch), :].astype(BF16)

        for b in range(BLOCKS):
            turned = tile(b)
            for piece in pieces:
                piece[b] = turned
        for n, piece in enumerate(pieces):
            for t in range(RIDE):
                piece[BLOCKS + t] = tile(BLOCKS + n * RIDE + t)

    return pl.pallas_call(
        kernel,
        in_specs=[VMEM],
        out_specs=[VMEM] * count,
        out_shape=[jax.ShapeDtypeStruct((PIECE, PLANE, BS), BF16)] * count,
        scratch_shapes=[pltpu.VMEM((PLANE * pitch, BS), F32)],
        compiler_params=PARAMS,
        cost_estimate=pl.CostEstimate(flops=600_000, bytes_accessed=2_000_000, transcendentals=0),
        name="turn",
    )(rows)


def relay_kernel(got, message):
    for i in range(PLANE):
        message[i, :BLOCKS] = got[:BLOCKS]
        message[i, BLOCKS:] = got[BLOCKS + i * RIDE : BLOCKS + (i + 1) * RIDE]


def relay(got):
    return pl.pallas_call(
        relay_kernel,
        in_specs=[VMEM],
        out_specs=VMEM,
        out_shape=jax.ShapeDtypeStruct((PLANE, PIECE, BS), BF16),
        compiler_params=PARAMS,
        cost_estimate=pl.CostEstimate(flops=0, bytes_accessed=700_000, transcendentals=0),
        name="relay",
    )(got)


def settle(pieces, flags, master, moment1, moment2, before):
    arrays = [a for piece in pieces for a in piece[1:]]
    aliased = list(before)

    def kernel(*refs):
        inputs, refs = refs[: len(arrays)], refs[len(arrays) :]
        flags, master, moment1, moment2 = refs[:4]
        refs = refs[4 + len(aliased) :]
        steps, outs, new, sems, new_sems = refs[0], refs[1:4], refs[4], refs[5], refs[6]
        z, core = lax.axis_index("z"), lax.axis_index("core")
        copies = []
        places = []
        for n, ref in enumerate(inputs):
            at = first_row(lax.rem(z + pieces[n // 2][0], 4), core if n % 2 == 0 else 1 - core)
            rows = pl.ds(pl.multiple_of(at, PLANE), PLANE)
            places.append(rows)
            copies.append(pltpu.make_async_copy(ref.at[pl.ds(0, BLOCKS)], steps.at[:, rows], sems.at[n]))
            copies[-1].start()
        for n, ref in enumerate(inputs):
            rows = places[n]
            for s in range(OWNCAP):
                tile = BLOCKS + n % 2 * OWNCAP + s
                totals = ref[tile].astype(F32) + ref[tile + RIDE // 2].astype(F32)
                old = [array[s, rows, :] for array in (master, moment1, moment2)]
                changed = flags[s : s + 1] > 0.5
                new1, new2, direction = adamw(totals, *old)
                new[0, s, rows] = jnp.where(changed, old[0] - LEARN_RATE * direction, old[0])
                new[1, s, rows] = jnp.where(changed, new1, old[1])
                new[2, s, rows] = jnp.where(changed, new2, old[2])
        for n in range(len(inputs)):
            rows = places[n]
            for array in range(3):
                for s in range(OWNCAP):
                    copies.append(
                        pltpu.make_async_copy(
                            new.at[array, s, rows], outs[array].at[s, rows], new_sems.at[n, array, s]
                        )
                    )
                    copies[-1].start()
        for copy in copies:
            copy.wait()

    slots = jax.ShapeDtypeStruct((OWNCAP, BS, BS), F32)
    return pl.pallas_call(
        kernel,
        in_specs=[VMEM] * (len(arrays) + 4) + [HBM] * len(aliased),
        out_specs=[HBM] * 4,
        out_shape=[jax.ShapeDtypeStruct((BLOCKS, BS, BS), BF16), slots, slots, slots],
        scratch_shapes=[
            pltpu.VMEM((3, OWNCAP, BS, BS), F32),
            pltpu.SemaphoreType.DMA((len(arrays),)),
            pltpu.SemaphoreType.DMA((len(arrays), 3, OWNCAP)),
        ],
        input_output_aliases={len(arrays) + 4 + n: n for n in range(len(aliased))},
        compiler_params=PARAMS,
        cost_estimate=pl.CostEstimate(flops=600_000, bytes_accessed=2_400_000, transcendentals=33_000),
        name="settle",
    )(*arrays, flags, master, moment1, moment2, *aliased)


RIGHT = [(i, (i + 1) % 4) for i in range(4)]
LEFT = [(i, (i + 3) % 4) for i in range(4)]
ACROSS = [(i, (i + 2) % 4) for i in range(4)]


def swap(piece):
    return lax.ppermute(piece, "core", [(0, 1), (1, 0)])


def local(grad, error, sel_blocks, row_bounds, col_bounds, master, moment1, moment2):
    send = pack(sel_blocks, grad, error, master, moment1, moment2)
    got = lax.all_to_all(send, ("row", "z", "core"), split_axis=0, concat_axis=0, tiled=True)
    slot_map, block_map, own_map = maps(row_bounds, col_bounds)
    error_out = feedback(sel_blocks, grad, error, 0, None)
    got, error_out = lax.optimization_barrier((got, error_out))
    message, across, flags = directions(got, slot_map, block_map, own_map)

    def exchange(message):
        rows = message.shape[1]
        got = lax.all_to_all(message.reshape(PLANE * rows, BS), "row", split_axis=0, concat_axis=0, tiled=True)
        return got.reshape(PLANE, rows, BS)

    message, error_out = lax.optimization_barrier((message, error_out))
    plane = exchange(message)
    far_message = relay(lax.ppermute(across, "z", ACROSS))
    error_out = feedback(sel_blocks, grad, error, 1, error_out)
    plane, far_message, error_out = lax.optimization_barrier((plane, far_message, error_out))
    mine, right, left = turn(plane)

    before = lax.ppermute(right, "z", RIGHT)
    after = lax.ppermute(left, "z", LEFT)
    mine_too = swap(mine)
    far_message, mine = lax.optimization_barrier((far_message, mine))
    far_plane = exchange(far_message)
    outs = settle([(0, mine, mine_too)], flags, master, moment1, moment2, ())
    before, after, far_plane, outs = lax.optimization_barrier((before, after, far_plane, outs))
    (far,) = turn(far_plane)
    before_too, after_too, far_too = swap(before), swap(after), swap(far)
    outs = settle([(3, before, before_too), (1, after, after_too)], flags, master, moment1, moment2, outs)
    far_too, outs = lax.optimization_barrier((far_too, outs))
    steps, *states = settle([(2, far, far_too)], flags, master, moment1, moment2, outs)
    return (error_out, *states, steps)


def solution(mesh):
    cores = Mesh(mesh.devices.reshape(N_ROW, N_COL // 2, 2), ("row", "z", "core"))
    split = P(("row", "z", "core"))
    return jax.shard_map(
        local,
        mesh=cores,
        in_specs=(split, split, split, P(), P(), split, split, split),
        out_specs=(split, split, split, split, P()),
        check_vma=False,
    )
```

```python
import jax
import jax.numpy as jnp
from jax import lax
from jax.experimental import pallas as pl
from jax.experimental.pallas import tpu as pltpu
from jax.sharding import Mesh
from jax.sharding import PartitionSpec as P

BS = 128
GC = 6
GR = 24
BLOCKS = 144
SEL = 7
OWNCAP = 2
N_ROW = 16
N_COL = 8
DEVICES = N_ROW * N_COL
PLANE = N_ROW
CHIPS = 4 * PLANE

MSG = 8
STATE_ROW = 4
INFO_ROW = 7
SCALE_LANE = 8
RIDE = 8
UNIT = 2.0**26
STEPS = 32767.0
ROOT_STEPS = 65535.0
ROOT_LOW = 32768.0

BETA_ONE = 0.9
BETA_TWO = 0.95
EPSILON = 1e-08
DECAY_RATE = 0.1
LEARN_RATE = 0.01
CORRECT_ONE = 1.0 - 0.9**10
CORRECT_TWO = 1.0 - 0.95**10

F32 = jnp.float32
BF16 = jnp.bfloat16
I32 = jnp.int32
SMEM = pl.BlockSpec(memory_space=pltpu.SMEM)
VMEM = pl.BlockSpec(memory_space=pltpu.VMEM)
HBM = pl.BlockSpec(memory_space=pltpu.HBM)
ANY = pl.BlockSpec(memory_space=pl.ANY)
MIB = 1024 * 1024
PARAMS = pltpu.CompilerParams(vmem_limit_bytes=16 * MIB)
ALONE = pltpu.CompilerParams(vmem_limit_bytes=64 * MIB)
NEARLY_ALONE = pltpu.CompilerParams(vmem_limit_bytes=61 * MIB)


def adamw(totals, master, moment1, moment2):
    averaged = totals / DEVICES
    first = BETA_ONE * moment1 + (1.0 - BETA_ONE) * averaged
    second = BETA_TWO * moment2 + (1.0 - BETA_TWO) * averaged * averaged
    direction = first / CORRECT_ONE / (jnp.sqrt(second / CORRECT_TWO) + EPSILON) + DECAY_RATE * master
    return first, second, direction


def three_terms(x):
    high = x.astype(BF16)
    rest = x - high.astype(F32)
    middle = rest.astype(BF16)
    low = (rest - middle.astype(F32)).astype(BF16)
    return high, middle, low


def first_row(z, core):
    return core * (BS // 2) + z * PLANE


def pack_kernel(sel_hbm, grad, error, master, moment1, moment2, send, sel, grads, errors, states, sel_sem, sems):
    fetch_sel = pltpu.make_async_copy(sel_hbm, sel, sel_sem)
    fetch_sel.start()
    held = [
        pltpu.make_async_copy(array, states.at[n], sems.at[2 * SEL + n])
        for n, array in enumerate((moment1, moment2, master))
    ]
    for copy in held:
        copy.start()
    fetch_sel.wait()
    chosen = []
    for k in range(SEL):
        at = jnp.minimum(sel[0, k], BLOCKS - 1)
        chosen.append(pltpu.make_async_copy(grad.at[at], grads.at[k], sems.at[k]))
        chosen.append(pltpu.make_async_copy(error.at[at], errors.at[k], sems.at[SEL + k]))
    for copy in chosen:
        copy.start()

    def put(row, block):
        for col in range(N_COL):
            at = first_row(col // 2, col % 2)
            send[pl.ds(col * MSG + row, PLANE, stride=N_COL * MSG), :] = block[at : at + PLANE]

    lane = lax.broadcasted_iota(I32, (BS, BS), 1)
    info = jnp.zeros((BS, BS), I32)
    for k in range(SEL):
        info = jnp.where(lane == k, sel[0, k], info)

    def coded(n, info, block, root=False):
        scale = jnp.maximum(jnp.ceil(jnp.max(jnp.abs(block), axis=1, keepdims=True) * UNIT), 1.0)
        info = jnp.where(lane == SCALE_LANE + n, scale.astype(I32), info)
        if root:
            return jnp.round(block * (ROOT_STEPS * UNIT / scale) - ROOT_LOW).astype(I32), info
        return jnp.round(block * (STEPS * UNIT / scale)).astype(I32), info

    def put_pair(row, first, second):
        put(row, lax.shift_left(first, 16) | (second & 0xFFFF))

    for n in range(3):
        held[n].wait()
        pair = []
        for s in range(OWNCAP):
            block = states[n, s]
            code, info = coded(SEL + OWNCAP * n + s, info, jnp.sqrt(block) if n == 1 else block, n == 1)
            pair.append(code)
        put_pair(STATE_ROW + n, *pair)
    pair = []
    for k in range(SEL):
        chosen[2 * k].wait()
        chosen[2 * k + 1].wait()
        code, info = coded(k, info, grads[k].astype(F32) + errors[k])
        pair.append(code)
        if len(pair) == 2:
            put_pair(k // 2, *pair)
            pair = []
    put_pair(SEL // 2, pair[0], jnp.zeros((BS, BS), I32))
    put(INFO_ROW, info)


def pack(sel, grad, error, master, moment1, moment2):
    return pl.pallas_call(
        pack_kernel,
        in_specs=[HBM] * 6,
        out_specs=VMEM,
        out_shape=jax.ShapeDtypeStruct((DEVICES * MSG, BS), I32),
        scratch_shapes=[
            pltpu.SMEM((1, SEL), I32),
            pltpu.VMEM((SEL, BS, BS), BF16),
            pltpu.VMEM((SEL, BS, BS), F32),
            pltpu.VMEM((3, OWNCAP, BS, BS), F32),
            pltpu.SemaphoreType.DMA,
            pltpu.SemaphoreType.DMA((2 * SEL + 3,)),
        ],
        compiler_params=ALONE,
        cost_estimate=pl.CostEstimate(flops=200_000, bytes_accessed=2_200_000, transcendentals=0),
        name="pack_rows",
    )(sel, grad, error, master, moment1, moment2)


def band(cuts, bands, positions):
    index = jnp.zeros_like(positions)
    start = jnp.zeros_like(positions)
    for k in range(1, bands):
        past = cuts[k] <= positions
        index = index + past.astype(I32)
        start = jnp.where(past, cuts[k], start)
    return index, start


FEED = 18


def feedback(sel, grad, error, part, before):
    steps = BLOCKS // FEED // 2

    def kernel(*refs):
        sel, grad, error, out = *refs[:3], refs[-1]

        def step(grad_blocks, error_blocks, out_blocks):
            first = (part * steps + pl.program_id(0)) * FEED
            for b in range(FEED):
                hit = sel[0, 0] == first + b
                for k in range(1, SEL):
                    hit = jnp.logical_or(hit, sel[0, k] == first + b)
                keep = 1.0 - hit.astype(F32)
                out_blocks[b] = (grad_blocks[b].astype(F32) + error_blocks[b]) * keep

        block = pl.BlockSpec((FEED, BS, BS), lambda i: (part * steps + i, 0, 0))
        pltpu.emit_pipeline(step, grid=(steps,), in_specs=[block, block], out_specs=[block])(grad, error, out)

    more = [] if before is None else [before]
    return pl.pallas_call(
        kernel,
        in_specs=[SMEM] + [HBM] * 2 + [HBM] * len(more),
        out_specs=HBM,
        out_shape=jax.ShapeDtypeStruct((BLOCKS, BS, BS), F32),
        input_output_aliases={3: 0} if more else {},
        compiler_params=NEARLY_ALONE,
        cost_estimate=pl.CostEstimate(flops=2_500_000, bytes_accessed=11_800_000, transcendentals=0),
        name="error_feedback",
    )(sel, grad, error, *more)


def maps_kernel(rows_ref, cols_ref, slot_map, block_map, own_map):
    block = lax.broadcasted_iota(I32, (BLOCKS, BS), 0)
    lane = lax.broadcasted_iota(I32, (BLOCKS, BS), 1)
    grid_row = block // GC
    grid_col = block - grid_row * GC
    row_band, row_start = band(rows_ref, N_ROW, grid_row)
    col_band, col_start = band(cols_ref, N_COL, grid_col)
    owner = row_band * N_COL + col_band
    slot = (grid_row - row_start) + (grid_col - col_start)
    for s in range(OWNCAP):
        slot_map[:, s * BS : (s + 1) * BS] = jnp.where((owner == lane) & (slot == s), 1.0, 0.0).astype(BF16)
    holder = lax.broadcasted_iota(I32, (RIDE * CHIPS, BS), 0)
    chip = holder // RIDE
    slot = holder % OWNCAP
    core = lax.axis_index("core")
    band_row = chip % PLANE
    at_z = lax.axis_index("z") + chip // PLANE
    at_z = jnp.where(at_z >= 4, at_z - 4, at_z)
    band_col = at_z * 2 + jnp.where(holder % 4 < OWNCAP, core, 1 - core)
    top = jnp.zeros_like(holder)
    end = jnp.zeros_like(holder)
    for k in range(N_ROW):
        top = jnp.where(band_row == k, rows_ref[k], top)
        end = jnp.where(band_row == k, rows_ref[k + 1], end)
    left = jnp.zeros_like(holder)
    right = jnp.zeros_like(holder)
    for k in range(N_COL):
        left = jnp.where(band_col == k, cols_ref[k], left)
        right = jnp.where(band_col == k, cols_ref[k + 1], right)
    at_row = top + slot
    target = jnp.where((at_row < end) & (left < right), at_row * GC + left, -1)
    lane = lax.broadcasted_iota(I32, (RIDE * CHIPS, BS), 1)
    for part in range(2):
        block_map[:, part * BS : (part + 1) * BS] = jnp.where(target == lane + part * BS, 1.0, 0.0).astype(BF16)
    band_row = lax.axis_index("row")
    band_col = 2 * lax.axis_index("z") + lax.axis_index("core")
    slot = lax.broadcasted_iota(I32, (16, 2 * BS), 0)
    at_row = rows_ref[band_row] + slot
    left = cols_ref[band_col]
    inside = (slot < OWNCAP) & (at_row < rows_ref[band_row + 1]) & (left < cols_ref[band_col + 1])
    lane = lax.broadcasted_iota(I32, (16, 2 * BS), 1)
    own_map[...] = jnp.where(inside & (at_row * GC + left == lane), 1.0, 0.0).astype(BF16)


def maps(row_bounds, col_bounds):
    return pl.pallas_call(
        maps_kernel,
        in_specs=[SMEM] * 2,
        out_specs=[VMEM] * 3,
        out_shape=[
            jax.ShapeDtypeStruct((BLOCKS, OWNCAP * BS), BF16),
            jax.ShapeDtypeStruct((RIDE * CHIPS, 2 * BS), BF16),
            jax.ShapeDtypeStruct((16, 2 * BS), BF16),
        ],
        compiler_params=PARAMS,
        cost_estimate=pl.CostEstimate(flops=500_000, bytes_accessed=300_000, transcendentals=0),
        name="slot_maps",
    )(row_bounds, col_bounds)


def directions_kernel(got, slot_map, block_map, own_map, message, across, flags):
    def rows(k):
        return got[pl.ds(k, DEVICES, stride=MSG), :]

    info = rows(INFO_ROW)

    def decoded(row, n):
        words = rows(row)
        for half in (lax.shift_right_arithmetic(words, 16), lax.shift_right_arithmetic(lax.shift_left(words, 16), 16)):
            if n < SEL or row > SEL // 2:
                scale = info[:, SCALE_LANE + n : SCALE_LANE + n + 1].astype(F32)
                if row == STATE_ROW + 1:
                    yield (half.astype(F32) + ROOT_LOW) * (scale * (1.0 / (ROOT_STEPS * UNIT)))
                else:
                    yield half.astype(F32) * (scale * (1.0 / (STEPS * UNIT)))
            n += 1

    ids = jnp.transpose(info.astype(F32))
    block = lax.broadcasted_iota(I32, (BLOCKS, DEVICES), 0).astype(F32)
    picks = jnp.concatenate(
        [jnp.where(ids[k : k + 1] == block, 1.0, 0.0).astype(BF16) for k in range(SEL)], axis=1
    )
    values = jnp.concatenate([value for row in range(STATE_ROW) for value in decoded(row, 2 * row)], axis=0)
    ones = jnp.ones((SEL * DEVICES, BS), BF16)
    sums = jnp.dot(picks, jnp.concatenate([*three_terms(values), ones], axis=1), preferred_element_type=F32)
    totals = (sums[:, :BS] + sums[:, BS : 2 * BS]) + sums[:, 2 * BS : 3 * BS]
    tallies = sums[:, 3 * BS :]

    states = []
    for array in range(3):
        held = jnp.concatenate(list(decoded(STATE_ROW + array, SEL + OWNCAP * array)), axis=0)
        states += three_terms(held)
    found = jnp.dot(slot_map[...], jnp.concatenate(states, axis=1), preferred_element_type=F32)
    term = [found[:, n * BS : (n + 1) * BS] for n in range(9)]
    moment1, root2, master = [(term[3 * a] + term[3 * a + 1]) + term[3 * a + 2] for a in range(3)]

    direction = adamw(totals, master, moment1, root2 * root2)[2]
    direction = jnp.where(tallies > 0.5, direction, 0.0).astype(BF16)
    padded = jnp.concatenate([totals, jnp.zeros((2 * BS - BLOCKS, BS), F32)], axis=0)
    sums = jnp.dot(block_map[...], jnp.concatenate(three_terms(padded), axis=1), preferred_element_type=F32)
    high, low, _ = three_terms((sums[:, :BS] + sums[:, BS : 2 * BS]) + sums[:, 2 * BS :])
    term = lax.broadcasted_iota(I32, (RIDE * CHIPS, BS), 0) % RIDE < RIDE // 2
    both = jnp.where(term, high.astype(F32), low.astype(F32)).astype(BF16)
    for i in range(PLANE):
        message[i, :BLOCKS] = direction
        for n, away in enumerate((0, 1, 3)):
            first = (away * PLANE + i) * RIDE
            message[i, BLOCKS + n * RIDE : BLOCKS + (n + 1) * RIDE] = both[first : first + RIDE]
    across[:BLOCKS] = direction
    across[BLOCKS:] = both[2 * PLANE * RIDE : 3 * PLANE * RIDE]

    padded = jnp.concatenate([tallies, jnp.zeros((2 * BS - BLOCKS, BS), F32)], axis=0).astype(BF16)
    flags[...] = jnp.dot(own_map[...], padded, preferred_element_type=F32)


def directions(got, slot_map, block_map, own_map):
    return pl.pallas_call(
        directions_kernel,
        in_specs=[VMEM] * 4,
        out_specs=[VMEM] * 3,
        out_shape=[
            jax.ShapeDtypeStruct((PLANE, BLOCKS + 3 * RIDE, BS), BF16),
            jax.ShapeDtypeStruct((BLOCKS + PLANE * RIDE, BS), BF16),
            jax.ShapeDtypeStruct((16, BS), F32),
        ],
        compiler_params=PARAMS,
        cost_estimate=pl.CostEstimate(flops=200_000_000, bytes_accessed=2_000_000, transcendentals=20_000),
        name="directions",
    )(got, slot_map, block_map, own_map)


PITCH = BLOCKS + 1


PIECE = BLOCKS + RIDE


def turn(rows):
    count = (rows.shape[1] - BLOCKS) // RIDE
    pitch = rows.shape[1] + 1

    def kernel(rows, *rest):
        pieces, scratch = rest[:-1], rest[-1]
        for chip in range(PLANE):
            scratch[pl.ds(chip * pitch, pitch - 1), :] = rows[chip].astype(F32)

        def tile(row):
            return scratch[pl.ds(row, PLANE, stride=pitch), :].astype(BF16)

        for b in range(BLOCKS):
            turned = tile(b)
            for piece in pieces:
                piece[b] = turned
        for n, piece in enumerate(pieces):
            for t in range(RIDE):
                piece[BLOCKS + t] = tile(BLOCKS + n * RIDE + t)

    return pl.pallas_call(
        kernel,
        in_specs=[VMEM],
        out_specs=[VMEM] * count,
        out_shape=[jax.ShapeDtypeStruct((PIECE, PLANE, BS), BF16)] * count,
        scratch_shapes=[pltpu.VMEM((PLANE * pitch, BS), F32)],
        compiler_params=PARAMS,
        cost_estimate=pl.CostEstimate(flops=600_000, bytes_accessed=2_000_000, transcendentals=0),
        name="turn",
    )(rows)


def relay_kernel(got, message):
    for i in range(PLANE):
        message[i, :BLOCKS] = got[:BLOCKS]
        message[i, BLOCKS:] = got[BLOCKS + i * RIDE : BLOCKS + (i + 1) * RIDE]


def relay(got):
    return pl.pallas_call(
        relay_kernel,
        in_specs=[VMEM],
        out_specs=VMEM,
        out_shape=jax.ShapeDtypeStruct((PLANE, PIECE, BS), BF16),
        compiler_params=PARAMS,
        cost_estimate=pl.CostEstimate(flops=0, bytes_accessed=700_000, transcendentals=0),
        name="relay",
    )(got)


def settle(pieces, flags, master, moment1, moment2, before):
    arrays = [a for piece in pieces for a in piece[1:]]
    aliased = list(before)

    def kernel(*refs):
        inputs, refs = refs[: len(arrays)], refs[len(arrays) :]
        flags, master, moment1, moment2 = refs[:4]
        refs = refs[4 + len(aliased) :]
        steps, outs, new, sems, new_sems = refs[0], refs[1:4], refs[4], refs[5], refs[6]
        z, core = lax.axis_index("z"), lax.axis_index("core")
        copies = []
        places = []
        for n, ref in enumerate(inputs):
            at = first_row(lax.rem(z + pieces[n // 2][0], 4), core if n % 2 == 0 else 1 - core)
            rows = pl.ds(pl.multiple_of(at, PLANE), PLANE)
            places.append(rows)
            copies.append(pltpu.make_async_copy(ref.at[pl.ds(0, BLOCKS)], steps.at[:, rows], sems.at[n]))
            copies[-1].start()
        for n, ref in enumerate(inputs):
            rows = places[n]
            for s in range(OWNCAP):
                tile = BLOCKS + n % 2 * OWNCAP + s
                totals = ref[tile].astype(F32) + ref[tile + RIDE // 2].astype(F32)
                old = [array[s, rows, :] for array in (master, moment1, moment2)]
                changed = flags[s : s + 1] > 0.5
                new1, new2, direction = adamw(totals, *old)
                new[0, s, rows] = jnp.where(changed, old[0] - LEARN_RATE * direction, old[0])
                new[1, s, rows] = jnp.where(changed, new1, old[1])
                new[2, s, rows] = jnp.where(changed, new2, old[2])
        for n in range(len(inputs)):
            rows = places[n]
            for array in range(3):
                for s in range(OWNCAP):
                    copies.append(
                        pltpu.make_async_copy(
                            new.at[array, s, rows], outs[array].at[s, rows], new_sems.at[n, array, s]
                        )
                    )
                    copies[-1].start()
        for copy in copies:
            copy.wait()

    slots = jax.ShapeDtypeStruct((OWNCAP, BS, BS), F32)
    return pl.pallas_call(
        kernel,
        in_specs=[VMEM] * (len(arrays) + 4) + [HBM] * len(aliased),
        out_specs=[HBM] * 4,
        out_shape=[jax.ShapeDtypeStruct((BLOCKS, BS, BS), BF16), slots, slots, slots],
        scratch_shapes=[
            pltpu.VMEM((3, OWNCAP, BS, BS), F32),
            pltpu.SemaphoreType.DMA((len(arrays),)),
            pltpu.SemaphoreType.DMA((len(arrays), 3, OWNCAP)),
        ],
        input_output_aliases={len(arrays) + 4 + n: n for n in range(len(aliased))},
        compiler_params=PARAMS,
        cost_estimate=pl.CostEstimate(flops=600_000, bytes_accessed=2_400_000, transcendentals=33_000),
        name="settle",
    )(*arrays, flags, master, moment1, moment2, *aliased)


RIGHT = [(i, (i + 1) % 4) for i in range(4)]
LEFT = [(i, (i + 3) % 4) for i in range(4)]
ACROSS = [(i, (i + 2) % 4) for i in range(4)]


def swap(piece):
    return lax.ppermute(piece, "core", [(0, 1), (1, 0)])


def local(grad, error, sel_blocks, row_bounds, col_bounds, master, moment1, moment2):
    send = pack(sel_blocks, grad, error, master, moment1, moment2)
    got = lax.all_to_all(send, ("row", "z", "core"), split_axis=0, concat_axis=0, tiled=True)
    slot_map, block_map, own_map = maps(row_bounds, col_bounds)
    error_out = feedback(sel_blocks, grad, error, 0, None)
    got, error_out = lax.optimization_barrier((got, error_out))
    message, across, flags = directions(got, slot_map, block_map, own_map)

    def exchange(message):
        rows = message.shape[1]
        got = lax.all_to_all(message.reshape(PLANE * rows, BS), "row", split_axis=0, concat_axis=0, tiled=True)
        return got.reshape(PLANE, rows, BS)

    message, error_out = lax.optimization_barrier((message, error_out))
    plane = exchange(message)
    far_message = relay(lax.ppermute(across, "z", ACROSS))
    error_out = feedback(sel_blocks, grad, error, 1, error_out)
    plane, far_message, error_out = lax.optimization_barrier((plane, far_message, error_out))
    mine, right, left = turn(plane)

    before = lax.ppermute(right, "z", RIGHT)
    after = lax.ppermute(left, "z", LEFT)
    mine_too = swap(mine)
    far_message, mine = lax.optimization_barrier((far_message, mine))
    far_plane = exchange(far_message)
    outs = settle([(0, mine, mine_too)], flags, master, moment1, moment2, ())
    before, after, outs = lax.optimization_barrier((before, after, outs))
    before_too, after_too = swap(before), swap(after)
    (far,) = turn(far_plane)
    far_too = swap(far)
    outs = settle([(3, before, before_too), (1, after, after_too)], flags, master, moment1, moment2, outs)
    far_too, outs = lax.optimization_barrier((far_too, outs))
    steps, *states = settle([(2, far, far_too)], flags, master, moment1, moment2, outs)
    return (error_out, *states, steps)


def solution(mesh):
    cores = Mesh(mesh.devices.reshape(N_ROW, N_COL // 2, 2), ("row", "z", "core"))
    split = P(("row", "z", "core"))
    return jax.shard_map(
        local,
        mesh=cores,
        in_specs=(split, split, split, P(), P(), split, split, split),
        out_specs=(split, split, split, split, P()),
        check_vma=False,
    )
```
